768 devices in a mesh: dom: 192 (over z, y, core), rep: 4 (over x).
Axes of the slice: x: 4, y: 8, z: 12, core: 2. Of those that a mesh axis runs over, the one named last changes fastest.
Arguments:
- features: bfloat16 [589824, 128], P('dom'), may hold values from -6 to 6
- w_self: bfloat16 [128, 256], replicated, may hold values from -0.5 to 0.5
- w_neigh: bfloat16 [128, 256], replicated, may hold values from -0.5 to 0.5
- bias: float32 [256], replicated, may hold values from -3 to 3
- cotangent: bfloat16 [589824, 256], P(('dom', 'rep')), may hold values from -6 to 6
- slot_source: int32 [4608, 8], P(('dom', 'rep')), may hold values from 0 to 59, as said below
- tile_masks: int32 [4608, 8, 128, 128], P(('dom', 'rep')), may hold values from 0 to 1, as said below
- panel_blocks: int32 [192, 6, 6], P('dom'), may hold values from 0 to 23
Outputs:
- activated: bfloat16 [589824, 256], P(('dom', 'rep'))
- grad_features: float32 [589824, 128], P(('dom', 'rep'))
- grad_self: float32 [128, 256], replicated
- grad_neigh: float32 [128, 256], replicated
- grad_bias: float32 [256], replicated
The draws below stay inside these ranges and needn't reach their ends.
Inputs may be any that keep to these rules, and one draw needn't show every extreme that they name: `slot_source`: slot 0 of each destination block names the block's own position in its partition; odd slots name received blocks, the other even slots own blocks of the partition. `tile_masks`: some nodes have no edges at all.
All inputs are finite; a program needn't handle non-finite values.
Results may differ from the reference program's by a relative error of at most 0.0047.
Values may be sent and summed in bfloat16 or wider, within the bound.
A program may use at most 64 MiB of HBM per device.

```python
import math
import jax
import jax.numpy as jnp
from jax import lax

F_IN = 128
HID = 256
TILE = 128
SLOTS = 8
ROUNDS = 3
PANEL = 6
PART_BLOCKS = 24
RECEIVED = 36
PARTITIONS = 192
BLOCKS = 4608
NODES = 589824


def draw_slot_source(key, part):
    key = jax.random.fold_in(key, 11)
    blocks = jnp.arange(BLOCKS, dtype=jnp.int32)
    local = blocks % PART_BLOCKS
    column = jnp.arange(SLOTS, dtype=jnp.int32)
    half = SLOTS // 2
    panel_pick = PART_BLOCKS + (local[:, None] * half + (column[None, :] - 1) // 2) % RECEIVED
    own_pick = jax.random.randint(key, (BLOCKS, SLOTS), 0, PART_BLOCKS)
    picks = jnp.where(column[None, :] % 2 == 1, panel_pick, own_pick)
    return jnp.where(column[None, :] == 0, local[:, None], picks).astype(jnp.int32)


def draw_tile_masks(key, part):
    key = jax.random.fold_in(key, 23)
    first, second, third = jax.random.split(key, 3)
    rate = jax.random.randint(first, (BLOCKS, 1, TILE, 1), 1, 120)
    lonely = jax.random.randint(second, (BLOCKS, 1, TILE, 1), 0, 40) == 0
    rate = jnp.where(lonely, 0, rate)
    roll = jax.random.randint(third, (BLOCKS, SLOTS, TILE, TILE), 0, 1000)
    return (roll < rate).astype(jnp.int32)


def plant(result, own_key, smallest, largest):
    shape = result.shape
    place = [jax.random.randint(jax.random.fold_in(own_key, axis), (), 0, shape[axis]) for axis in range(len(shape))]
    result = result.at[tuple(place)].set(smallest)
    longest = shape.index(max(shape))
    place[longest] = (place[longest] + 1) % shape[longest]
    return result.at[tuple(place)].set(largest)


def block_scale(own_key, extent, cuts, smallest, top_value):
    loudness, own = 1.0, jax.random.fold_in(own_key, 6)
    for axis_at, blocks in cuts:
        steps = jnp.exp(jax.random.uniform(jax.random.fold_in(own, axis_at), (blocks,), jnp.float32, smallest / len(cuts), top_value / len(cuts)))
        loudness = loudness * jnp.repeat(steps, extent[axis_at] // blocks).reshape([-1 if axis == axis_at else 1 for axis in range(len(extent))])
    return loudness


def centred(own_key, shape, width, reach, shards=(), kind=jnp.bfloat16):
    loudness = block_scale(own_key, shape, shards, -0.22, 0.18) if shards else 1.0
    entries = jax.random.normal(own_key, shape, jnp.float32) * width * loudness
    return jnp.minimum(jnp.maximum(entries, -reach), reach).astype(kind)


def setup_inputs(seed: int = 0) -> dict:
    seeds = jax.random.split(jax.random.key(seed), 9)
    return {
        "features": centred(seeds[0], (NODES, F_IN), 1.0, 6.0, ((0, 192),)),
        "w_self": centred(seeds[1], (F_IN, HID), F_IN ** -0.5, 0.5),
        "w_neigh": centred(seeds[2], (F_IN, HID), F_IN ** -0.5, 0.5),
        "bias": centred(seeds[3], (HID,), 0.5, 3.0, (), jnp.float32),
        "cotangent": centred(seeds[4], (NODES, HID), 1.0, 6.0, ((0, 768),)),
        "slot_source": draw_slot_source(jax.random.fold_in(seeds[8], 71), 0),
        "tile_masks": draw_tile_masks(jax.random.fold_in(seeds[8], 71), 0),
        "panel_blocks": plant(jax.random.randint(seeds[7], (PARTITIONS, 2 * ROUNDS, PANEL), 0, PART_BLOCKS), jax.random.fold_in(seeds[7], 1), 0, PART_BLOCKS - 1).astype(jnp.int32),
    }


def reference(features, w_self, w_neigh, bias, cotangent, slot_source, tile_masks, panel_blocks):
    parts = PARTITIONS
    turns = 2 * ROUNDS
    x_all = features.reshape(parts, PART_BLOCKS, TILE, F_IN)
    shifts = jnp.array([t // 2 + 1 if t % 2 == 0 else -(t // 2 + 1) for t in range(turns)], jnp.int32)
    senders = (jnp.arange(parts, dtype=jnp.int32)[:, None] - shifts[None, :]) % parts
    turn_ids = jnp.arange(turns, dtype=jnp.int32)[None, :]
    sent_idx = panel_blocks[senders, turn_ids]
    panels = x_all[senders[:, :, None], sent_idx]
    slots_p = slot_source.reshape(parts, PART_BLOCKS, SLOTS)
    masks_p = tile_masks.reshape(parts, PART_BLOCKS, SLOTS, TILE, TILE)

    def forward_part(args):
        own, recv, slots, masks = args
        sources = jnp.concatenate([own, recv.reshape(RECEIVED, TILE, F_IN)], 0)
        tiles = sources[slots].astype(jnp.float32)
        return jnp.einsum('dsij,dsjf->dif', masks.astype(jnp.float32), tiles)
    agg_sum = lax.map(forward_part, (x_all, panels, slots_p, masks_p)).reshape(NODES, F_IN)
    degree = jnp.maximum(lax.optimization_barrier(jnp.sum(tile_masks, axis=(1, 3))), 1).astype(jnp.float32).reshape(NODES, 1)
    agg = (agg_sum / degree).astype(jnp.bfloat16)
    z = jnp.dot(features, w_self, preferred_element_type=jnp.float32) + jnp.dot(agg, w_neigh, preferred_element_type=jnp.float32) + bias
    activated = jax.nn.silu(z).astype(jnp.bfloat16)
    sig = jax.nn.sigmoid(z)
    dz = cotangent.astype(jnp.float32) * (sig * (1.0 + z * (1.0 - sig)))
    dz_b = dz.astype(jnp.bfloat16)
    scale = 1.0 / math.sqrt(NODES)
    grad_self = jnp.dot(features.T, dz_b, preferred_element_type=jnp.float32) * scale
    grad_neigh = jnp.dot(agg.T, dz_b, preferred_element_type=jnp.float32) * scale
    grad_bias = lax.optimization_barrier(jnp.sum(dz, axis=0)) * scale
    q = (jnp.dot(dz_b, w_neigh.T, preferred_element_type=jnp.float32) / degree).astype(jnp.bfloat16)
    q_p = q.reshape(parts, PART_BLOCKS, TILE, F_IN)

    def backward_part(args):
        qb, slots, masks = args
        contrib = jnp.einsum('dsij,dif->dsjf', masks.astype(jnp.float32), qb.astype(jnp.float32))
        hot = (slots[:, :, None] == jnp.arange(PART_BLOCKS + RECEIVED, dtype=jnp.int32)[None, None, :]).astype(jnp.float32)
        return jnp.einsum('dsk,dsjf->kjf', hot, contrib, precision=lax.Precision.HIGHEST)
    src_grad = lax.map(backward_part, (q_p, slots_p, masks_p))
    own_grad = src_grad[:, :PART_BLOCKS]
    returned = src_grad[:, PART_BLOCKS:].reshape(parts, turns, PANEL, TILE, F_IN)
    own_grad = own_grad.at[senders[:, :, None], sent_idx].add(returned)
    grad_features = jnp.dot(dz_b, w_self.T, preferred_element_type=jnp.float32) + own_grad.reshape(NODES, F_IN)
    return (activated, grad_features, grad_self, grad_neigh, grad_bias)
```

```python
import functools
import math

import jax
import jax.numpy as jnp
from jax import lax
from jax.experimental import pallas as pl
from jax.experimental.pallas import tpu as pltpu
from jax.sharding import PartitionSpec as P

MESH = pl.DeviceIdType.MESH
F32 = jnp.float32
BF16 = jnp.bfloat16
CONTRACT_ROWS = (((0,), (0,)), ((), ()))
CONTRACT_LANES = (((1,), (1,)), ((), ()))


def dot(a, b):
    return jnp.dot(a, b, preferred_element_type=F32)


def chain(values):
    lane = lax.broadcasted_iota(jnp.int32, (1, 128), 1)
    listed = jnp.full((1, 128), -1, jnp.int32)
    for j, value in enumerate(values):
        listed = jnp.where(lane == j, value, listed)
    prev = jnp.zeros((1, 128), jnp.int32)
    last = jnp.zeros((1, 128), jnp.int32)
    for i, value in enumerate(values):
        prev = jnp.where((listed == value) & (lane > i), i + 1, prev)
        last = jnp.where(lane == value, i + 1, last)
    return prev, last


def kernel(
    sizes, feat_hbm, w_self_hbm, w_neigh_hbm, bias_hbm, cot_hbm, masks_hbm, slot_ref, panel_ref,
    act_hbm, gf_hbm, gs_ref, gn_ref, gb_ref,
    feat, w_self, w_neigh, bias, cot, masks, mask_b, mask_t, inv, z0, agg_even, agg_b, dz_b, q_b, act, gf,
    panel_out, recv, grad_out, returned, chain_odd, chain_even, chain_back, own, own_mine, x_pass, x_near,
    got_pass, got_near, idx_v, idx_s,
    r1_out, r1_in, r2_out, r2_in, r3_out, r3_in, r4, r5,
    in_sem, mask_sem, idx_sem, out_sem, fwd_send, fwd_recv, back_send, back_recv, x_send, x_recv,
    s1_send, s1_recv, s2_send, s2_recv, s3_send, s3_recv, s4_send, s4_recv, s5_send, s5_recv,
):
    doms, reps, subs, offsets, nodes = sizes
    layers = doms // subs
    turns = len(offsets)
    panel = panel_ref.shape[2]
    blocks, slots = slot_ref.shape
    half = slots // 2
    part_blocks, tile, width = feat.shape
    hidden = w_self.shape[1]
    rows_each = width // subs
    dom = lax.axis_index("dom")
    rep = lax.axis_index("rep")
    layer = dom // subs
    sub = dom % subs

    def received(i, k):
        return jnp.maximum(slot_ref[i, 2 * k + 1] - part_blocks, 0)

    loads = [
        pltpu.make_async_copy(feat_hbm, feat, in_sem.at[0]),
        pltpu.make_async_copy(w_self_hbm, w_self, in_sem.at[1]),
        pltpu.make_async_copy(w_neigh_hbm, w_neigh, in_sem.at[2]),
        pltpu.make_async_copy(bias_hbm, bias, in_sem.at[3]),
        pltpu.make_async_copy(cot_hbm, cot, in_sem.at[4]),
    ]
    for load in loads:
        load.start()
    for i in range(blocks):
        pltpu.make_async_copy(masks_hbm.at[i], masks.at[i], mask_sem.at[i]).start()

    barrier = pltpu.get_barrier_semaphore()

    def greet(d, r):
        pl.semaphore_signal(barrier, inc=1, device_id=(d, r), device_id_type=MESH)

    for offset in offsets:
        greet((dom + offset + doms) % doms, rep)
    for k in range(1, reps):
        greet(dom, (rep + k) % reps)

    def greet_sub(k, carry):
        greet(layer * subs + (sub + k) % subs, rep)
        return carry

    def greet_layer(k, carry):
        greet(((layer + k) % layers) * subs + sub, rep)
        return carry

    lax.fori_loop(1, subs, greet_sub, 0)
    lax.fori_loop(1, layers, greet_layer, 0)

    loads[0].wait()
    for t in range(turns):
        for i in range(panel):
            panel_out[t * panel + i] = feat[panel_ref[0, t, i]]
    pl.semaphore_wait(barrier, turns + reps - 1 + subs - 1 + layers - 1)

    def to_dom(t, source, target, send, recv_sem, offset):
        part = pl.ds(t * panel, panel)
        return pltpu.make_async_remote_copy(
            src_ref=source.at[part], dst_ref=target.at[part], send_sem=send.at[t], recv_sem=recv_sem.at[t],
            device_id=((dom + offset + doms) % doms, rep), device_id_type=MESH,
        )

    sends = [to_dom(t, panel_out, recv, fwd_send, fwd_recv, offsets[t]) for t in range(turns)]
    for t in reversed(range(turns)):
        sends[t].start()

    odd = [received(i, k) for i in range(blocks) for k in range(half)]
    even = [slot_ref[i, 2 * k] for i in range(blocks) for k in range(half)]
    back = [panel_ref[0, t, i] for t in range(turns) for i in range(panel)]
    for at, values in enumerate((odd, even, back)):
        prev, last = chain(values)
        idx_v[2 * at : 2 * at + 1, :] = prev
        idx_v[2 * at + 1 : 2 * at + 2, :] = last
    idx_v[6:8, :] = jnp.zeros((2, 128), jnp.int32)
    idx_copy = pltpu.make_async_copy(idx_v, idx_s, idx_sem)
    idx_copy.start()
    chain_odd[0] = jnp.zeros((tile, width), F32)
    chain_even[0] = jnp.zeros((tile, width), F32)
    chain_back[0] = jnp.zeros((tile, width), F32)
    loads[1].wait()
    loads[2].wait()
    loads[3].wait()

    def prepare(i, carry):
        pltpu.make_async_copy(masks_hbm.at[i], masks.at[i], mask_sem.at[i]).wait()
        total = jnp.zeros((tile, tile), F32)
        aggregate = jnp.zeros((tile, width), F32)
        for k in range(slots):
            mask = masks[i, k].astype(F32)
            total = total + mask
            mask = mask.astype(BF16)
            mask_b[i, k] = mask
            mask_t[i, k] = mask.T
            if k % 2 == 0:
                aggregate = aggregate + dot(mask, feat[slot_ref[i, k]])
        agg_even[i] = aggregate
        degree = jnp.maximum(jnp.sum(total, axis=1, keepdims=True), 1.0)
        inv[i] = jnp.broadcast_to(1.0 / degree, (tile, width))
        z0[i] = dot(feat[rep * blocks + i], w_self[...]) + bias[...]
        return carry

    lax.fori_loop(0, blocks, prepare, 0)
    loads[4].wait()
    idx_copy.wait()
    for send in sends:
        send.wait_recv()

    def forward(i, bias_total):
        aggregate = agg_even[i]
        for k in range(half):
            aggregate = aggregate + dot(mask_b[i, 2 * k + 1], recv[received(i, k)])
        agg = (aggregate * inv[i]).astype(BF16)
        agg_b[i] = agg
        z = z0[i] + dot(agg, w_neigh[...])
        sig = lax.logistic(z)
        act[i] = (z * sig).astype(BF16)
        dz = cot[i].astype(F32) * (sig * (1.0 + z * (1.0 - sig)))
        dzb = dz.astype(BF16)
        dz_b[i] = dzb
        q = lax.dot_general(dzb, w_neigh[...], CONTRACT_LANES, preferred_element_type=F32)
        q = (q * inv[i]).astype(BF16)
        q_b[i] = q
        for k in range(half):
            at = i * half + k
            chain_odd[at + 1] = chain_odd[idx_s[0, at]] + dot(mask_t[i, 2 * k + 1], q)
        return bias_total + jnp.sum(dz, axis=0, keepdims=True)

    bias_total = lax.fori_loop(0, blocks, forward, jnp.zeros((1, hidden), F32))
    act_copy = pltpu.make_async_copy(act, act_hbm, out_sem.at[0])
    act_copy.start()
    returns = [to_dom(t, grad_out, returned, back_send, back_recv, -offsets[t]) for t in range(turns)]
    for t in reversed(range(turns)):
        for i in range(panel):
            grad_out[t * panel + i] = chain_odd[idx_s[1, t * panel + i]].astype(BF16)
        returns[t].start()

    bias_rows = 8

    def weights(i, carry):
        part_self, part_neigh = carry
        dzb = dz_b[i]
        part_self = part_self + lax.dot_general(
            feat[rep * blocks + i], dzb, CONTRACT_ROWS, preferred_element_type=F32
        )
        part_neigh = part_neigh + lax.dot_general(agg_b[i], dzb, CONTRACT_ROWS, preferred_element_type=F32)
        return part_self, part_neigh

    zero = jnp.zeros((width, hidden), F32)
    part_self, part_neigh = lax.fori_loop(0, blocks, weights, (zero, zero))
    for at, part in enumerate((part_self, part_neigh)):
        for c in range(2):
            r1_out[2 * at + c, 0:width] = part[:, c * 128 : (c + 1) * 128]
    row = lax.broadcasted_iota(jnp.int32, (bias_rows, 128), 0)
    bias_tile = jnp.where(row == 0, bias_total[:, :128], jnp.where(row == 1, bias_total[:, 128:], 0.0))
    for at in range(reps):
        r1_out[at, width : width + bias_rows] = bias_tile

    def stage_1(k):
        peer = (rep + k) % reps
        return pltpu.make_async_remote_copy(
            src_ref=r1_out.at[peer], dst_ref=r1_in.at[k - 1], send_sem=s1_send.at[k - 1], recv_sem=s1_recv.at[k - 1],
            device_id=(dom, peer), device_id_type=MESH,
        )

    for k in range(1, reps):
        stage_1(k).start()

    def backward(i, carry):
        q = q_b[i]
        for k in range(half):
            at = i * half + k
            chain_even[at + 1] = chain_even[idx_s[2, at]] + dot(mask_t[i, 2 * k], q)
        gf[i] = lax.dot_general(dz_b[i], w_self[...], CONTRACT_LANES, preferred_element_type=F32)
        return carry

    lax.fori_loop(0, blocks, backward, 0)

    for k in range(1, reps):
        stage_1(k).wait_recv()
    summed = r1_out[rep]
    for k in range(1, reps):
        summed = summed + r1_in[k - 1]
    for j in range(subs):
        r2_out[j, 0:rows_each] = summed[j * rows_each : (j + 1) * rows_each]
        r2_out[j, rows_each : rows_each + bias_rows] = summed[width : width + bias_rows]

    def stage_2(k):
        peer = (sub + k) % subs
        return pltpu.make_async_remote_copy(
            src_ref=r2_out.at[peer], dst_ref=r2_in.at[k - 1], send_sem=s2_send.at[k - 1], recv_sem=s2_recv.at[k - 1],
            device_id=(layer * subs + peer, rep), device_id_type=MESH,
        )

    def stage_3(k):
        peer = (layer + k) % layers
        return pltpu.make_async_remote_copy(
            src_ref=r3_out, dst_ref=r3_in.at[k - 1], send_sem=s3_send.at[k - 1], recv_sem=s3_recv.at[k - 1],
            device_id=(peer * subs + sub, rep), device_id_type=MESH,
        )

    def stage_4(k):
        peer = (sub + k) % subs
        return pltpu.make_async_remote_copy(
            src_ref=r4.at[sub], dst_ref=r4.at[sub], send_sem=s4_send.at[k - 1], recv_sem=s4_recv.at[k - 1],
            device_id=(layer * subs + peer, rep), device_id_type=MESH,
        )

    def stage_5(k):
        peer = (rep + k) % reps
        return pltpu.make_async_remote_copy(
            src_ref=r5.at[rep], dst_ref=r5.at[rep], send_sem=s5_send.at[k - 1], recv_sem=s5_recv.at[k - 1],
            device_id=(dom, peer), device_id_type=MESH,
        )

    def start_all(stage, count):
        def step(k, carry):
            stage(k).start()
            return carry

        lax.fori_loop(1, count, step, 0)

    def receive_all(stage, count):
        def step(k, carry):
            stage(k).wait_recv()
            return carry

        lax.fori_loop(1, count, step, 0)

    def finish_all(stage, count):
        def step(k, carry):
            stage(k).wait_send()
            return carry

        lax.fori_loop(1, count, step, 0)

    start_all(stage_2, subs)
    receive_all(stage_2, subs)
    summed = r2_out[sub]
    for k in range(1, subs):
        summed = summed + r2_in[k - 1]
    r3_out[...] = summed
    start_all(stage_3, layers)

    def take(t):
        returns[t].wait_recv()
        for i in range(panel):
            at = t * panel + i
            chain_back[at + 1] = chain_back[idx_s[4, at]] + returned[at].astype(F32)

    order = list(range(turns))
    for t in order[: turns // 2]:
        take(t)
    receive_all(stage_3, layers)
    summed = r3_out[...]
    for k in range(1, layers):
        summed = summed + r3_in[k - 1]
    r4[sub] = summed[0:rows_each]
    final_bias = summed[rows_each : rows_each + bias_rows]
    start_all(stage_4, subs)
    for t in order[turns // 2 :]:
        take(t)

    right, left, across = (rep + 1) % reps, (rep + 3) % reps, (rep + 2) % reps
    part = blocks // 2

    def owned(block):
        return chain_even[idx_s[3, block]] + chain_back[idx_s[5, block]]

    def to_rep(source, target, at, peer):
        return pltpu.make_async_remote_copy(
            src_ref=source, dst_ref=target, send_sem=x_send.at[at], recv_sem=x_recv.at[at],
            device_id=(dom, peer), device_id_type=MESH,
        )

    passing = [to_rep(x_pass.at[s], got_pass.at[s], s, (right, left)[s]) for s in range(2)]
    for s in range(2):
        for j in range(part):
            x_pass[s, j] = owned(across * blocks + s * part + j).astype(BF16)
        passing[s].start()
    near = [
        [to_rep(x_near.at[s, h], got_near.at[s, h], 2 + 2 * s + h, (right, left)[s]) for h in range(2)]
        for s in range(2)
    ]
    for s in range(2):
        peer = (right, left)[s]
        for j in range(part):
            x_near[s, 0, j] = owned(peer * blocks + (1 - s) * part + j).astype(BF16)
        near[s][0].start()
    for s in range(2):
        peer = (right, left)[s]
        for j in range(part):
            own[s, j] = owned(peer * blocks + s * part + j)
    for s in range(2):
        passing[s].wait_recv()
        for j in range(part):
            x_near[s, 1, j] = (own[s, j] + got_pass[s, j].astype(F32)).astype(BF16)
        near[s][1].start()
    for j in range(blocks):
        own_mine[j] = owned(rep * blocks + j) + gf[j]

    receive_all(stage_4, subs)
    for j in range(subs):
        r5[rep, j * rows_each : (j + 1) * rows_each] = r4[j]
    for k in range(1, reps):
        stage_5(k).start()

    for s in range(2):
        near[s][0].wait_recv()
    for s in range(2):
        near[s][1].wait_recv()
    for s in range(2):
        for j in range(part):
            at = s * part + j
            gf[at] = own_mine[at] + got_near[0, 1 - s, j].astype(F32) + got_near[1, s, j].astype(F32)
    gf_copy = pltpu.make_async_copy(gf, gf_hbm, out_sem.at[1])
    gf_copy.start()

    scale = 1.0 / math.sqrt(nodes)
    for k in range(1, reps):
        stage_5(k).wait_recv()
    for c in range(2):
        gs_ref[:, c * 128 : (c + 1) * 128] = r5[c] * scale
        gn_ref[:, c * 128 : (c + 1) * 128] = r5[2 + c] * scale
        gb_ref[:, c * 128 : (c + 1) * 128] = final_bias[c : c + 1] * scale

    for send in sends + returns:
        send.wait_send()
    for s in range(2):
        passing[s].wait_send()
        for h in range(2):
            near[s][h].wait_send()
    finish_all(stage_1, reps)
    finish_all(stage_2, subs)
    finish_all(stage_3, layers)
    finish_all(stage_4, subs)
    finish_all(stage_5, reps)
    act_copy.wait()
    gf_copy.wait()


def per_device(sizes, features, w_self, w_neigh, bias, cotangent, slot_source, tile_masks, panel_blocks):
    doms, reps, subs, offsets, nodes = sizes
    layers = doms // subs
    blocks, slots, tile, _ = tile_masks.shape
    width, hidden = w_self.shape
    part_blocks = features.shape[0] // tile
    turns, panel = panel_blocks.shape[1:]
    tiles = blocks * slots // 2
    rows_each = width // subs
    part = blocks // 2
    dma = pltpu.SemaphoreType.DMA
    any_space = pl.BlockSpec(memory_space=pl.ANY)
    vmem = pl.BlockSpec(memory_space=pltpu.VMEM)
    smem = pl.BlockSpec(memory_space=pltpu.SMEM)
    block = (tile, width)
    scratch = [
        pltpu.VMEM((part_blocks,) + block, BF16),
        pltpu.VMEM((width, hidden), BF16),
        pltpu.VMEM((width, hidden), BF16),
        pltpu.VMEM((1, hidden), F32),
        pltpu.VMEM((blocks, tile, hidden), BF16),
        pltpu.VMEM((blocks, slots, tile, tile), jnp.int32),
        pltpu.VMEM((blocks, slots, tile, tile), BF16),
        pltpu.VMEM((blocks, slots, tile, tile), BF16),
        pltpu.VMEM((blocks,) + block, F32),
        pltpu.VMEM((blocks, tile, hidden), F32),
        pltpu.VMEM((blocks,) + block, F32),
        pltpu.VMEM((blocks,) + block, BF16),
        pltpu.VMEM((blocks, tile, hidden), BF16),
        pltpu.VMEM((blocks,) + block, BF16),
        pltpu.VMEM((blocks, tile, hidden), BF16),
        pltpu.VMEM((blocks,) + block, F32),
        pltpu.VMEM((turns * panel,) + block, BF16),
        pltpu.VMEM((turns * panel,) + block, BF16),
        pltpu.VMEM((turns * panel,) + block, BF16),
        pltpu.VMEM((turns * panel,) + block, BF16),
        pltpu.VMEM((tiles + 1,) + block, F32),
        pltpu.VMEM((tiles + 1,) + block, F32),
        pltpu.VMEM((turns * panel + 1,) + block, F32),
        pltpu.VMEM((2, part) + block, F32),
        pltpu.VMEM((blocks,) + block, F32),
        pltpu.VMEM((2, part) + block, BF16),
        pltpu.VMEM((2, 2, part) + block, BF16),
        pltpu.VMEM((2, part) + block, BF16),
        pltpu.VMEM((2, 2, part) + block, BF16),
        pltpu.VMEM((8, 128), jnp.int32),
        pltpu.SMEM((8, 128), jnp.int32),
        pltpu.VMEM((reps, width + 8, 128), F32),
        pltpu.VMEM((reps - 1, width + 8, 128), F32),
        pltpu.VMEM((subs, rows_each + 8, 128), F32),
        pltpu.VMEM((subs - 1, rows_each + 8, 128), F32),
        pltpu.VMEM((rows_each + 8, 128), F32),
        pltpu.VMEM((layers - 1, rows_each + 8, 128), F32),
        pltpu.VMEM((subs, rows_each, 128), F32),
        pltpu.VMEM((reps, width, 128), F32),
        dma((5,)), dma((blocks,)), dma, dma((2,)),
        dma((turns,)), dma((turns,)), dma((turns,)), dma((turns,)), dma((6,)), dma((6,)),
        dma((reps - 1,)), dma((reps - 1,)), dma((subs - 1,)), dma((subs - 1,)),
        dma((layers - 1,)), dma((layers - 1,)), dma((subs - 1,)), dma((subs - 1,)),
        dma((reps - 1,)), dma((reps - 1,)),
    ]
    act, gf, gs, gn, gb = pl.pallas_call(
        functools.partial(kernel, sizes),
        out_shape=(
            jax.ShapeDtypeStruct((blocks, tile, hidden), BF16),
            jax.ShapeDtypeStruct((blocks,) + block, F32),
            jax.ShapeDtypeStruct((width, hidden), F32),
            jax.ShapeDtypeStruct((width, hidden), F32),
            jax.ShapeDtypeStruct((1, hidden), F32),
        ),
        in_specs=[any_space] * 6 + [smem] * 2,
        out_specs=(any_space, any_space, vmem, vmem, vmem),
        scratch_shapes=scratch,
        compiler_params=pltpu.CompilerParams(
            collective_id=0, has_side_effects=True, vmem_limit_bytes=48 * 1024 * 1024
        ),
    )(
        features.reshape((part_blocks,) + block),
        w_self,
        w_neigh,
        bias.reshape(1, hidden),
        cotangent.reshape(blocks, tile, hidden),
        tile_masks,
        slot_source,
        panel_blocks,
    )
    return (
        act.reshape(blocks * tile, hidden),
        gf.reshape(blocks * tile, width),
        gs,
        gn,
        gb.reshape(hidden),
    )


def solution(mesh):
    doms, reps = mesh.shape["dom"], mesh.shape["rep"]
    subs = 16 if doms % 16 == 0 else doms // 2
    offsets = (1, -1, 2, -2, 3, -3)
    in_specs = (
        P("dom", None),
        P(),
        P(),
        P(),
        P(("dom", "rep"), None),
        P(("dom", "rep"), None),
        P(("dom", "rep"), None, None, None),
        P("dom", None, None),
    )
    out_specs = (P(("dom", "rep"), None), P(("dom", "rep"), None), P(), P(), P())

    def step(features, *rest):
        nodes = features.shape[0] * doms
        return per_device((doms, reps, subs, offsets, nodes), features, *rest)

    return jax.shard_map(step, mesh=mesh, in_specs=in_specs, out_specs=out_specs, check_vma=False)
```

```python
import functools
import math

import jax
import jax.numpy as jnp
from jax import lax
from jax.experimental import pallas as pl
from jax.experimental.pallas import tpu as pltpu
from jax.sharding import PartitionSpec as P

MESH = pl.DeviceIdType.MESH
F32 = jnp.float32
BF16 = jnp.bfloat16
CONTRACT_ROWS = (((0,), (0,)), ((), ()))
CONTRACT_LANES = (((1,), (1,)), ((), ()))


def dot(a, b):
    return jnp.dot(a, b, preferred_element_type=F32)


def chain(values):
    lane = lax.broadcasted_iota(jnp.int32, (1, 128), 1)
    listed = jnp.full((1, 128), -1, jnp.int32)
    for j, value in enumerate(values):
        listed = jnp.where(lane == j, value, listed)
    prev = jnp.zeros((1, 128), jnp.int32)
    last = jnp.zeros((1, 128), jnp.int32)
    for i, value in enumerate(values):
        prev = jnp.where((listed == value) & (lane > i), i + 1, prev)
        last = jnp.where(lane == value, i + 1, last)
    return prev, last


def kernel(
    sizes, feat_hbm, w_self_hbm, w_neigh_hbm, bias_hbm, cot_hbm, masks_hbm, slot_ref, panel_ref,
    act_hbm, gf_hbm, gs_ref, gn_ref, gb_ref,
    feat, w_self, w_neigh, bias, cot, masks, mask_b, mask_t, inv, z0, agg_even, agg_b, dz_b, q_b, act, gf,
    panel_out, recv, grad_out, returned, chain_odd, chain_even, chain_back, own, own_mine, x_pass, x_near,
    got_pass, got_near, idx_v, idx_s,
    r1_out, r1_in, r2_out, r2_in, r3_out, r3_in, r4, r5,
    in_sem, mask_sem, idx_sem, out_sem, fwd_send, fwd_recv, back_send, back_recv, x_send, x_recv,
    s1_send, s1_recv, s2_send, s2_recv, s3_send, s3_recv, s4_send, s4_recv, s5_send, s5_recv,
):
    doms, reps, subs, offsets, nodes = sizes
    layers = doms // subs
    turns = len(offsets)
    panel = panel_ref.shape[2]
    blocks, slots = slot_ref.shape
    half = slots // 2
    part_blocks, tile, width = feat.shape
    hidden = w_self.shape[1]
    ways = 2 * reps
    ranks = subs // 2
    half_rows = width // 2
    rows_each = half_rows // ranks
    dom = lax.axis_index("dom")
    rep = lax.axis_index("rep")
    layer = dom // subs
    sub = dom % subs
    rank = sub // 2
    core = dom % 2
    other = 1 - 2 * core
    piece = rep * 2 + core

    def received(i, k):
        return jnp.maximum(slot_ref[i, 2 * k + 1] - part_blocks, 0)

    loads = [
        pltpu.make_async_copy(feat_hbm, feat, in_sem.at[0]),
        pltpu.make_async_copy(w_self_hbm, w_self, in_sem.at[1]),
        pltpu.make_async_copy(w_neigh_hbm, w_neigh, in_sem.at[2]),
        pltpu.make_async_copy(bias_hbm, bias, in_sem.at[3]),
        pltpu.make_async_copy(cot_hbm, cot, in_sem.at[4]),
    ]
    for load in loads:
        load.start()
    for i in range(blocks):
        pltpu.make_async_copy(masks_hbm.at[i], masks.at[i], mask_sem.at[i]).start()

    barrier = pltpu.get_barrier_semaphore()

    def greet(d, r):
        pl.semaphore_signal(barrier, inc=1, device_id=(d, r), device_id_type=MESH)

    for offset in offsets:
        greet((dom + offset + doms) % doms, rep)
    for m in range(1, ways):
        greet(dom + other * (m // reps), (rep + m) % reps)
    for k in range(1, ranks):
        greet(layer * subs + ((rank + k) % ranks) * 2 + core, rep)
    for k in range(1, layers):
        greet(((layer + k) % layers) * subs + sub, rep)

    loads[0].wait()
    for t in range(turns):
        for i in range(panel):
            panel_out[t * panel + i] = feat[panel_ref[t, 0, i]]
    pl.semaphore_wait(barrier, turns + ways - 1 + ranks - 1 + layers - 1)

    def to_dom(t, source, target, send, recv_sem, offset):
        part = pl.ds(t * panel, panel)
        return pltpu.make_async_remote_copy(
            src_ref=source.at[part], dst_ref=target.at[part], send_sem=send.at[t], recv_sem=recv_sem.at[t],
            device_id=((dom + offset + doms) % doms, rep), device_id_type=MESH,
        )

    sends = [to_dom(t, panel_out, recv, fwd_send, fwd_recv, offsets[t]) for t in range(turns)]
    for t in reversed(range(turns)):
        sends[t].start()

    odd = [received(i, k) for i in range(blocks) for k in range(half)]
    even = [slot_ref[i, 2 * k] for i in range(blocks) for k in range(half)]
    back = [panel_ref[t, 0, i] for t in range(turns) for i in range(panel)]
    for at, values in enumerate((odd, even, back)):
        prev, last = chain(values)
        idx_v[2 * at : 2 * at + 1, :] = prev
        idx_v[2 * at + 1 : 2 * at + 2, :] = last
    idx_v[6:8, :] = jnp.zeros((2, 128), jnp.int32)
    idx_copy = pltpu.make_async_copy(idx_v, idx_s, idx_sem)
    idx_copy.start()
    chain_odd[0] = jnp.zeros((tile, width), F32)
    chain_even[0] = jnp.zeros((tile, width), F32)
    chain_back[0] = jnp.zeros((tile, width), F32)
    loads[1].wait()
    loads[2].wait()
    loads[3].wait()

    def prepare(i, carry):
        pltpu.make_async_copy(masks_hbm.at[i], masks.at[i], mask_sem.at[i]).wait()
        total = jnp.zeros((tile, tile), F32)
        aggregate = jnp.zeros((tile, width), F32)
        for k in range(slots):
            mask = masks[i, k].astype(F32)
            total = total + mask
            mask = mask.astype(BF16)
            mask_b[i, k] = mask
            mask_t[i, k] = mask.T
            if k % 2 == 0:
                aggregate = aggregate + dot(mask, feat[slot_ref[i, k]])
        agg_even[i] = aggregate
        degree = jnp.maximum(jnp.sum(total, axis=1, keepdims=True), 1.0)
        inv[i] = jnp.broadcast_to(1.0 / degree, (tile, width))
        z0[i] = dot(feat[rep * blocks + i], w_self[...]) + bias[...]
        return carry

    lax.fori_loop(0, blocks, prepare, 0)
    loads[4].wait()
    idx_copy.wait()
    for send in sends:
        send.wait_recv()

    def forward(i, bias_total):
        aggregate = agg_even[i]
        for k in range(half):
            aggregate = aggregate + dot(mask_b[i, 2 * k + 1], recv[received(i, k)])
        agg = (aggregate * inv[i]).astype(BF16)
        agg_b[i] = agg
        z = z0[i] + dot(agg, w_neigh[...])
        sig = lax.logistic(z)
        act[i] = (z * sig).astype(BF16)
        dz = cot[i].astype(F32) * (sig * (1.0 + z * (1.0 - sig)))
        dzb = dz.astype(BF16)
        dz_b[i] = dzb
        q = lax.dot_general(dzb, w_neigh[...], CONTRACT_LANES, preferred_element_type=F32)
        q = (q * inv[i]).astype(BF16)
        q_b[i] = q
        for k in range(half):
            at = i * half + k
            chain_odd[at + 1] = chain_odd[idx_s[0, at]] + dot(mask_t[i, 2 * k + 1], q)
        return bias_total + jnp.sum(dz, axis=0, keepdims=True)

    bias_total = lax.fori_loop(0, blocks, forward, jnp.zeros((1, hidden), F32))
    act_copy = pltpu.make_async_copy(act, act_hbm, out_sem.at[0])
    act_copy.start()
    returns = [to_dom(t, grad_out, returned, back_send, back_recv, -offsets[t]) for t in range(turns)]
    for t in reversed(range(turns)):
        for i in range(panel):
            grad_out[t * panel + i] = chain_odd[idx_s[1, t * panel + i]].astype(BF16)
        returns[t].start()

    bias_rows = 8

    def weights(i, carry):
        part_self, part_neigh = carry
        dzb = dz_b[i]
        part_self = part_self + lax.dot_general(
            feat[rep * blocks + i], dzb, CONTRACT_ROWS, preferred_element_type=F32
        )
        part_neigh = part_neigh + lax.dot_general(agg_b[i], dzb, CONTRACT_ROWS, preferred_element_type=F32)
        return part_self, part_neigh

    zero = jnp.zeros((width, hidden), F32)
    part_self, part_neigh = lax.fori_loop(0, blocks, weights, (zero, zero))
    row = lax.broadcasted_iota(jnp.int32, (bias_rows, 128), 0)
    bias_tile = jnp.where(row == 0, bias_total[:, :128], jnp.where(row == 1, bias_total[:, 128:], 0.0))
    for at, part in enumerate((part_self, part_neigh)):
        for c in range(2):
            for h in range(2):
                to = (2 * at + c) * 2 + h
                r1_out[to, 0:half_rows] = part[h * half_rows : (h + 1) * half_rows, c * 128 : (c + 1) * 128]
                r1_out[to, half_rows : half_rows + bias_rows] = bias_tile

    def near_by(m):
        return dom + other * (m // reps), (rep + m) % reps

    def stage_1(m):
        peer, peer_rep = near_by(m)
        return pltpu.make_async_remote_copy(
            src_ref=r1_out.at[peer_rep * 2 + peer % 2], dst_ref=r1_in.at[m - 1],
            send_sem=s1_send.at[m - 1], recv_sem=s1_recv.at[m - 1],
            device_id=(peer, peer_rep), device_id_type=MESH,
        )

    def stage_2(k):
        peer = (rank + k) % ranks
        return pltpu.make_async_remote_copy(
            src_ref=r2_out.at[peer], dst_ref=r2_in.at[k - 1], send_sem=s2_send.at[k - 1], recv_sem=s2_recv.at[k - 1],
            device_id=(layer * subs + peer * 2 + core, rep), device_id_type=MESH,
        )

    def stage_3(k):
        peer = (layer + k) % layers
        return pltpu.make_async_remote_copy(
            src_ref=r3_out, dst_ref=r3_in.at[k - 1], send_sem=s3_send.at[k - 1], recv_sem=s3_recv.at[k - 1],
            device_id=(peer * subs + sub, rep), device_id_type=MESH,
        )

    def stage_4(k):
        peer = (rank + k) % ranks
        return pltpu.make_async_remote_copy(
            src_ref=r4.at[rank], dst_ref=r4.at[rank], send_sem=s4_send.at[k - 1], recv_sem=s4_recv.at[k - 1],
            device_id=(layer * subs + peer * 2 + core, rep), device_id_type=MESH,
        )

    def stage_5(m):
        peer, peer_rep = near_by(m)
        return pltpu.make_async_remote_copy(
            src_ref=r5.at[piece], dst_ref=r5.at[piece], send_sem=s5_send.at[m - 1], recv_sem=s5_recv.at[m - 1],
            device_id=(peer, peer_rep), device_id_type=MESH,
        )

    def start_all(stage, count):
        for k in range(1, count):
            stage(k).start()

    def receive_all(stage, count):
        for k in range(1, count):
            stage(k).wait_recv()

    def finish_all(stage, count):
        for k in range(1, count):
            stage(k).wait_send()

    start_all(stage_1, ways)

    def backward(i, carry):
        q = q_b[i]
        for k in range(half):
            at = i * half + k
            chain_even[at + 1] = chain_even[idx_s[2, at]] + dot(mask_t[i, 2 * k], q)
        gf[i] = lax.dot_general(dz_b[i], w_self[...], CONTRACT_LANES, preferred_element_type=F32)
        return carry

    lax.fori_loop(0, blocks, backward, 0)

    receive_all(stage_1, ways)
    summed = r1_out[piece]
    for m in range(1, ways):
        summed = summed + r1_in[m - 1]
    for j in range(ranks):
        r2_out[j, 0:rows_each] = summed[j * rows_each : (j + 1) * rows_each]
        r2_out[j, rows_each : rows_each + bias_rows] = summed[half_rows : half_rows + bias_rows]
    start_all(stage_2, ranks)
    receive_all(stage_2, ranks)
    summed = r2_out[rank]
    for k in range(1, ranks):
        summed = summed + r2_in[k - 1]
    r3_out[...] = summed
    start_all(stage_3, layers)

    def take(t):
        returns[t].wait_recv()
        for i in range(panel):
            at = t * panel + i
            chain_back[at + 1] = chain_back[idx_s[4, at]] + returned[at].astype(F32)

    order = list(range(turns))
    for t in order[: turns // 2]:
        take(t)
    receive_all(stage_3, layers)
    summed = r3_out[...]
    for k in range(1, layers):
        summed = summed + r3_in[k - 1]
    r4[rank] = summed[0:rows_each]
    final_bias = summed[rows_each : rows_each + bias_rows]
    start_all(stage_4, ranks)
    for t in order[turns // 2 :]:
        take(t)

    right, left, across = (rep + 1) % reps, (rep + 3) % reps, (rep + 2) % reps
    part = blocks // 2

    def owned(block):
        return chain_even[idx_s[3, block]] + chain_back[idx_s[5, block]]

    def to_rep(source, target, at, peer):
        return pltpu.make_async_remote_copy(
            src_ref=source, dst_ref=target, send_sem=x_send.at[at], recv_sem=x_recv.at[at],
            device_id=(dom, peer), device_id_type=MESH,
        )

    passing = [to_rep(x_pass.at[s], got_pass.at[s], s, (right, left)[s]) for s in range(2)]
    for s in range(2):
        for j in range(part):
            x_pass[s, j] = owned(across * blocks + s * part + j).astype(BF16)
        passing[s].start()
    near = [
        [to_rep(x_near.at[s, h], got_near.at[s, h], 2 + 2 * s + h, (right, left)[s]) for h in range(2)]
        for s in range(2)
    ]
    for s in range(2):
        peer = (right, left)[s]
        for j in range(part):
            x_near[s, 0, j] = owned(peer * blocks + (1 - s) * part + j).astype(BF16)
        near[s][0].start()
    for s in range(2):
        peer = (right, left)[s]
        for j in range(part):
            own[s, j] = owned(peer * blocks + s * part + j)
    for s in range(2):
        passing[s].wait_recv()
        for j in range(part):
            x_near[s, 1, j] = (own[s, j] + got_pass[s, j].astype(F32)).astype(BF16)
        near[s][1].start()
    for j in range(blocks):
        own_mine[j] = owned(rep * blocks + j) + gf[j]

    receive_all(stage_4, ranks)
    r5[piece] = r4[...].reshape(half_rows, 128).astype(BF16)
    start_all(stage_5, ways)

    for s in range(2):
        near[s][0].wait_recv()
    for s in range(2):
        near[s][1].wait_recv()
    for s in range(2):
        for j in range(part):
            at = s * part + j
            gf[at] = own_mine[at] + got_near[0, 1 - s, j].astype(F32) + got_near[1, s, j].astype(F32)
    gf_copy = pltpu.make_async_copy(gf, gf_hbm, out_sem.at[1])
    gf_copy.start()

    scale = 1.0 / math.sqrt(nodes)
    receive_all(stage_5, ways)
    for c in range(2):
        columns = slice(c * 128, (c + 1) * 128)
        for h in range(2):
            rows = slice(h * half_rows, (h + 1) * half_rows)
            gs_ref[rows, columns] = r5[c * 2 + h].astype(F32) * scale
            gn_ref[rows, columns] = r5[(2 + c) * 2 + h].astype(F32) * scale
        gb_ref[:, columns] = final_bias[c : c + 1] * scale

    for send in sends + returns:
        send.wait_send()
    for s in range(2):
        passing[s].wait_send()
        for h in range(2):
            near[s][h].wait_send()
    finish_all(stage_1, ways)
    finish_all(stage_2, ranks)
    finish_all(stage_3, layers)
    finish_all(stage_4, ranks)
    finish_all(stage_5, ways)
    act_copy.wait()
    gf_copy.wait()


def write_out(*refs):
    count = (len(refs) - 1) // 3
    given, results, held, sem = refs[:count], refs[count : 2 * count], refs[2 * count : 3 * count], refs[-1]
    reads = [pltpu.make_async_copy(given[i], held[i], sem.at[0, i]) for i in range(count)]
    writes = [pltpu.make_async_copy(held[i], results[i], sem.at[1, i]) for i in range(count)]
    for read in reads:
        read.start()
    for read, write in zip(reads, writes):
        read.wait()
        write.start()
    for write in writes:
        write.wait()


def per_device(sizes, features, w_self, w_neigh, bias, cotangent, slot_source, tile_masks, panel_blocks):
    doms, reps, subs, offsets, nodes = sizes
    layers = doms // subs
    blocks, slots, tile, _ = tile_masks.shape
    width, hidden = w_self.shape
    part_blocks = features.shape[0] // tile
    turns, panel = panel_blocks.shape[1:]
    tiles = blocks * slots // 2
    ways, ranks, half_rows = 2 * reps, subs // 2, width // 2
    rows_each = half_rows // ranks
    part = blocks // 2
    dma = pltpu.SemaphoreType.DMA
    any_space = pl.BlockSpec(memory_space=pl.ANY)
    vmem = pl.BlockSpec(memory_space=pltpu.VMEM)
    smem = pl.BlockSpec(memory_space=pltpu.SMEM)
    block = (tile, width)
    scratch = [
        pltpu.VMEM((part_blocks,) + block, BF16),
        pltpu.VMEM((width, hidden), BF16),
        pltpu.VMEM((width, hidden), BF16),
        pltpu.VMEM((1, hidden), F32),
        pltpu.VMEM((blocks, tile, hidden), BF16),
        pltpu.VMEM((blocks, slots, tile, tile), jnp.int32),
        pltpu.VMEM((blocks, slots, tile, tile), BF16),
        pltpu.VMEM((blocks, slots, tile, tile), BF16),
        pltpu.VMEM((blocks,) + block, F32),
        pltpu.VMEM((blocks, tile, hidden), F32),
        pltpu.VMEM((blocks,) + block, F32),
        pltpu.VMEM((blocks,) + block, BF16),
        pltpu.VMEM((blocks, tile, hidden), BF16),
        pltpu.VMEM((blocks,) + block, BF16),
        pltpu.VMEM((blocks, tile, hidden), BF16),
        pltpu.VMEM((blocks,) + block, F32),
        pltpu.VMEM((turns * panel,) + block, BF16),
        pltpu.VMEM((turns * panel,) + block, BF16),
        pltpu.VMEM((turns * panel,) + block, BF16),
        pltpu.VMEM((turns * panel,) + block, BF16),
        pltpu.VMEM((tiles + 1,) + block, F32),
        pltpu.VMEM((tiles + 1,) + block, F32),
        pltpu.VMEM((turns * panel + 1,) + block, F32),
        pltpu.VMEM((2, part) + block, F32),
        pltpu.VMEM((blocks,) + block, F32),
        pltpu.VMEM((2, part) + block, BF16),
        pltpu.VMEM((2, 2, part) + block, BF16),
        pltpu.VMEM((2, part) + block, BF16),
        pltpu.VMEM((2, 2, part) + block, BF16),
        pltpu.VMEM((8, 128), jnp.int32),
        pltpu.SMEM((8, 128), jnp.int32),
        pltpu.VMEM((ways, half_rows + 8, 128), F32),
        pltpu.VMEM((ways - 1, half_rows + 8, 128), F32),
        pltpu.VMEM((ranks, rows_each + 8, 128), F32),
        pltpu.VMEM((ranks - 1, rows_each + 8, 128), F32),
        pltpu.VMEM((rows_each + 8, 128), F32),
        pltpu.VMEM((layers - 1, rows_each + 8, 128), F32),
        pltpu.VMEM((ranks, rows_each, 128), F32),
        pltpu.VMEM((ways, half_rows, 128), BF16),
        dma((5,)), dma((blocks,)), dma, dma((2,)),
        dma((turns,)), dma((turns,)), dma((turns,)), dma((turns,)), dma((6,)), dma((6,)),
        dma((ways - 1,)), dma((ways - 1,)), dma((ranks - 1,)), dma((ranks - 1,)),
        dma((layers - 1,)), dma((layers - 1,)), dma((ranks - 1,)), dma((ranks - 1,)),
        dma((ways - 1,)), dma((ways - 1,)),
    ]
    results = pl.pallas_call(
        functools.partial(kernel, sizes),
        out_shape=(
            jax.ShapeDtypeStruct((blocks, tile, hidden), BF16),
            jax.ShapeDtypeStruct((blocks,) + block, F32),
            jax.ShapeDtypeStruct((width, hidden), F32),
            jax.ShapeDtypeStruct((width, hidden), F32),
            jax.ShapeDtypeStruct((1, hidden), F32),
        ),
        in_specs=[any_space] * 6 + [smem] * 2,
        out_specs=(any_space, any_space, vmem, vmem, vmem),
        scratch_shapes=scratch,
        compiler_params=pltpu.CompilerParams(
            collective_id=0, has_side_effects=True, vmem_limit_bytes=63 * 1024 * 1024
        ),
    )(
        features.reshape((part_blocks,) + block),
        w_self,
        w_neigh,
        bias.reshape(1, hidden),
        cotangent.reshape(blocks, tile, hidden),
        tile_masks,
        slot_source,
        panel_blocks.transpose(1, 0, 2),
    )
    act, gf, gs, gn, gb = pl.pallas_call(
        write_out,
        out_shape=tuple(jax.ShapeDtypeStruct(x.shape, x.dtype) for x in results),
        in_specs=[any_space] * len(results),
        out_specs=(any_space,) * len(results),
        scratch_shapes=[pltpu.VMEM(x.shape, x.dtype) for x in results] + [dma((2, len(results)))],
        compiler_params=pltpu.CompilerParams(vmem_limit_bytes=63 * 1024 * 1024),
    )(*results)
    return (
        act.reshape(blocks * tile, hidden),
        gf.reshape(blocks * tile, width),
        gs,
        gn,
        gb.reshape(hidden),
    )


def solution(mesh):
    doms, reps = mesh.shape["dom"], mesh.shape["rep"]
    subs = 16 if doms % 16 == 0 else doms // 2
    offsets = (1, -1, 2, -2, 3, -3)
    in_specs = (
        P("dom", None),
        P(),
        P(),
        P(),
        P(("dom", "rep"), None),
        P(("dom", "rep"), None),
        P(("dom", "rep"), None, None, None),
        P("dom", None, None),
    )
    out_specs = (P(("dom", "rep"), None), P(("dom", "rep"), None), P(), P(), P())

    def step(features, *rest):
        nodes = features.shape[0] * doms
        return per_device((doms, reps, subs, offsets, nodes), features, *rest)

    return jax.shard_map(step, mesh=mesh, in_specs=in_specs, out_specs=out_specs, check_vma=False)
```

```python
import functools
import math

import jax
import jax.numpy as jnp
from jax import lax
from jax.experimental import pallas as pl
from jax.experimental.pallas import tpu as pltpu
from jax.sharding import PartitionSpec as P

LATE = (4, 5)
UNROLL = 2
MESH = pl.DeviceIdType.MESH
F32 = jnp.float32
BF16 = jnp.bfloat16
CONTRACT_ROWS = (((0,), (0,)), ((), ()))
CONTRACT_LANES = (((1,), (1,)), ((), ()))


def dot(a, b):
    return jnp.dot(a, b, preferred_element_type=F32)


def chain(values):
    lane = lax.broadcasted_iota(jnp.int32, (1, 128), 1)
    listed = jnp.full((1, 128), -1, jnp.int32)
    for j, value in enumerate(values):
        listed = jnp.where(lane == j, value, listed)
    prev = jnp.zeros((1, 128), jnp.int32)
    last = jnp.zeros((1, 128), jnp.int32)
    for i, value in enumerate(values):
        prev = jnp.where((listed == value) & (lane > i), i + 1, prev)
        last = jnp.where(lane == value, i + 1, last)
    return prev, last


def kernel(
    sizes, feat_hbm, w_self_hbm, w_neigh_hbm, bias_hbm, cot_hbm, masks_hbm, slot_ref, panel_ref,
    act_hbm, gf_hbm, gs_ref, gn_ref, gb_ref,
    feat, w_self, w_neigh, bias, cot, masks, mask_b, mask_t, inv, z0, agg_even, feat_t, agg_t, dz_b, q_b, act, gf,
    panel_out, recv, grad_out, returned, chain_odd, chain_even, chain_back, own, own_mine, x_pass, x_near,
    got_pass, got_near, idx_v, idx_s,
    r1_out, r1_in, r2_out, r2_in, r3_out, r3_in, r4, r5,
    in_sem, mask_sem, idx_sem, out_sem, fwd_send, fwd_recv, far_send, far_recv, hand_send, hand_recv, back_send, back_recv, x_send, x_recv,
    s1_send, s1_recv, s2_send, s2_recv, s3_send, s3_recv, s4_send, s4_recv, s5_send, s5_recv,
):
    doms, reps, subs, offsets, nodes = sizes
    layers = doms // subs
    turns = len(offsets)
    panel = panel_ref.shape[2]
    blocks, slots = slot_ref.shape
    half = slots // 2
    part_blocks, tile, width = feat.shape
    hidden = w_self.shape[1]
    ways = 2 * reps
    ranks = subs // 2
    half_rows = width // 2
    rows_each = half_rows // ranks
    dom = lax.axis_index("dom")
    rep = lax.axis_index("rep")
    layer = dom // subs
    sub = dom % subs
    rank = sub // 2
    core = dom % 2
    other = 1 - 2 * core
    piece = rep * 2 + core

    def received(i, k):
        return jnp.maximum(slot_ref[i, 2 * k + 1] - part_blocks, 0)

    def columns_of(i):
        return pl.ds(pl.multiple_of(i * tile, tile), tile)

    loads = [
        pltpu.make_async_copy(feat_hbm, feat, in_sem.at[0]),
        pltpu.make_async_copy(w_self_hbm, w_self, in_sem.at[1]),
        pltpu.make_async_copy(w_neigh_hbm, w_neigh, in_sem.at[2]),
        pltpu.make_async_copy(bias_hbm, bias, in_sem.at[3]),
        pltpu.make_async_copy(cot_hbm, cot, in_sem.at[4]),
    ]
    for load in loads:
        load.start()
    for i in range(blocks):
        pltpu.make_async_copy(masks_hbm.at[i], masks.at[i], mask_sem.at[i]).start()

    barrier = pltpu.get_barrier_semaphore()

    def greet(d, r):
        pl.semaphore_signal(barrier, inc=1, device_id=(d, r), device_id_type=MESH)

    for offset in offsets:
        greet((dom + offset + doms) % doms, rep)
    for m in range(1, ways):
        greet(dom + other * (m // reps), (rep + m) % reps)
    for k in range(1, ranks):
        greet(layer * subs + ((rank + k) % ranks) * 2 + core, rep)
    for k in range(1, layers):
        greet(((layer + k) % layers) * subs + sub, rep)

    loads[0].wait()
    for t in range(turns):
        for i in range(panel):
            panel_out[t * panel + i] = feat[panel_ref[t, 0, i]]
    pl.semaphore_wait(barrier, turns + ways - 1 + ranks - 1 + layers - 1)

    def to_dom(t, source, target, send, recv_sem, offset, count=panel):
        part = pl.ds(t * panel, count)
        return pltpu.make_async_remote_copy(
            src_ref=source.at[part], dst_ref=target.at[part], send_sem=send.at[t], recv_sem=recv_sem.at[t],
            device_id=((dom + offset + doms) % doms, rep), device_id_type=MESH,
        )

    far = [t for t in range(turns) if abs(offsets[t]) == 3]
    common = panel - reps

    def to_far(n, source, target, send, recv_sem, way):
        mine = far[n] * panel + common + rep
        return pltpu.make_async_remote_copy(
            src_ref=source.at[mine], dst_ref=target.at[mine], send_sem=send.at[n], recv_sem=recv_sem.at[n],
            device_id=((dom + way * offsets[far[n]] + doms) % doms, rep), device_id_type=MESH,
        )

    def hand_on(n, k):
        mine = far[n] * panel + common + rep
        at = n * (reps - 1) + k - 1
        return pltpu.make_async_remote_copy(
            src_ref=recv.at[mine], dst_ref=recv.at[mine], send_sem=hand_send.at[at], recv_sem=hand_recv.at[at],
            device_id=(dom, (rep + k) % reps), device_id_type=MESH,
        )

    shared = [to_far(n, panel_out, recv, far_send, far_recv, 1) for n in range(len(far))]
    sends = [
        to_dom(t, panel_out, recv, fwd_send, fwd_recv, offsets[t], common if t in far else panel) for t in range(turns)
    ]
    for send in shared:
        send.start()
    for t in reversed(range(turns)):
        sends[t].start()
    odd = [received(i, k) for i in range(blocks) for k in range(half)]
    even = [slot_ref[i, 2 * k] for i in range(blocks) for k in range(half)]
    back = [panel_ref[t, 0, i] for t in range(turns) for i in range(panel)]
    for at, values in enumerate((odd, even, back)):
        prev, last = chain(values)
        idx_v[2 * at : 2 * at + 1, :] = prev
        idx_v[2 * at + 1 : 2 * at + 2, :] = last
    idx_v[6:8, :] = jnp.zeros((2, 128), jnp.int32)
    idx_copy = pltpu.make_async_copy(idx_v, idx_s, idx_sem)
    idx_copy.start()
    chain_odd[0] = jnp.zeros((tile, width), F32)
    chain_even[0] = jnp.zeros((tile, width), F32)
    chain_back[0] = jnp.zeros((tile, width), F32)
    for n in range(len(far)):
        shared[n].wait_recv()
        for k in range(1, reps):
            hand_on(n, k).start()

    loads[1].wait()
    loads[2].wait()
    loads[3].wait()

    def prepare(i, carry):
        pltpu.make_async_copy(masks_hbm.at[i], masks.at[i], mask_sem.at[i]).wait()
        total = jnp.zeros((tile, tile), F32)
        aggregate = jnp.zeros((tile, width), F32)
        for k in range(slots):
            mask = masks[i, k].astype(F32)
            total = total + mask
            mask = mask.astype(BF16)
            mask_b[i, k] = mask
            mask_t[i, k] = mask.T
            if k % 2 == 0:
                aggregate = aggregate + dot(mask, feat[slot_ref[i, k]])
        agg_even[i] = aggregate
        degree = jnp.maximum(jnp.sum(total, axis=1, keepdims=True), 1.0)
        inv[i] = jnp.broadcast_to(1.0 / degree, (tile, width))
        mine = feat[rep * blocks + i]
        feat_t[:, columns_of(i)] = mine.T
        z0[i] = dot(mine, w_self[...]) + bias[...]
        return carry

    lax.fori_loop(0, blocks, prepare, 0, unroll=UNROLL)
    loads[4].wait()
    idx_copy.wait()
    for send in sends:
        send.wait_recv()
    for n in range(len(far)):
        for k in range(1, reps):
            hand_on(n, k).wait_recv()

    def forward(i, bias_total):
        aggregate = agg_even[i]
        for k in range(half):
            aggregate = aggregate + dot(mask_b[i, 2 * k + 1], recv[received(i, k)])
        agg = (aggregate * inv[i]).astype(BF16)
        agg_t[:, columns_of(i)] = agg.T
        z = z0[i] + dot(agg, w_neigh[...])
        sig = lax.logistic(z)
        act[i] = (z * sig).astype(BF16)
        dz = cot[i].astype(F32) * (sig * (1.0 + z * (1.0 - sig)))
        dzb = dz.astype(BF16)
        dz_b[i] = dzb
        q = lax.dot_general(dzb, w_neigh[...], CONTRACT_LANES, preferred_element_type=F32)
        q = (q * inv[i]).astype(BF16)
        q_b[i] = q
        return bias_total + jnp.sum(dz, axis=0, keepdims=True)

    bias_total = lax.fori_loop(0, blocks, forward, jnp.zeros((1, hidden), F32), unroll=UNROLL)
    act_copy = pltpu.make_async_copy(act, act_hbm, out_sem.at[0])
    act_copy.start()

    bias_rows = 8
    packed_rows = 16
    dz_all = dz_b[...].reshape(blocks * tile, hidden)
    row = lax.broadcasted_iota(jnp.int32, (packed_rows, 128), 0)
    bias_high = bias_total.astype(BF16).astype(F32)
    bias_low = bias_total - bias_high
    bias_tile = jnp.zeros((packed_rows, 128), F32)
    for at, line in enumerate((bias_high, bias_low)):
        for c in range(2):
            bias_tile = jnp.where(row == 2 * at + c, line[:, c * 128 : (c + 1) * 128], bias_tile)
    bias_tile = bias_tile.astype(BF16)
    for at, left_side in enumerate((feat_t, agg_t)):
        part = dot(left_side[...], dz_all).astype(BF16)
        for c in range(2):
            for h in range(2):
                to = (2 * at + c) * 2 + h
                r1_out[to, 0:half_rows] = part[h * half_rows : (h + 1) * half_rows, c * 128 : (c + 1) * 128]
                r1_out[to, half_rows : half_rows + packed_rows] = bias_tile

    def near_by(m):
        return dom + other * (m // reps), (rep + m) % reps

    def stage_1(m):
        peer, peer_rep = near_by(m)
        return pltpu.make_async_remote_copy(
            src_ref=r1_out.at[peer_rep * 2 + peer % 2], dst_ref=r1_in.at[m - 1],
            send_sem=s1_send.at[m - 1], recv_sem=s1_recv.at[m - 1],
            device_id=(peer, peer_rep), device_id_type=MESH,
        )

    def stage_2(k):
        peer = (rank + k) % ranks
        return pltpu.make_async_remote_copy(
            src_ref=r2_out.at[peer], dst_ref=r2_in.at[k - 1], send_sem=s2_send.at[k - 1], recv_sem=s2_recv.at[k - 1],
            device_id=(layer * subs + peer * 2 + core, rep), device_id_type=MESH,
        )

    def stage_3(k):
        peer = (layer + k) % layers
        return pltpu.make_async_remote_copy(
            src_ref=r3_out, dst_ref=r3_in.at[k - 1], send_sem=s3_send.at[k - 1], recv_sem=s3_recv.at[k - 1],
            device_id=(peer * subs + sub, rep), device_id_type=MESH,
        )

    def stage_4(k):
        peer = (rank + k) % ranks
        return pltpu.make_async_remote_copy(
            src_ref=r4.at[rank], dst_ref=r4.at[rank], send_sem=s4_send.at[k - 1], recv_sem=s4_recv.at[k - 1],
            device_id=(layer * subs + peer * 2 + core, rep), device_id_type=MESH,
        )

    def stage_5(m):
        peer, peer_rep = near_by(m)
        return pltpu.make_async_remote_copy(
            src_ref=r5.at[piece], dst_ref=r5.at[piece], send_sem=s5_send.at[m - 1], recv_sem=s5_recv.at[m - 1],
            device_id=(peer, peer_rep), device_id_type=MESH,
        )

    def start_all(stage, count):
        for k in range(1, count):
            stage(k).start()

    def receive_all(stage, count):
        for k in range(1, count):
            stage(k).wait_recv()

    def finish_all(stage, count):
        for k in range(1, count):
            stage(k).wait_send()

    start_all(stage_1, ways)

    def backward_received(i, carry):
        q = q_b[i]
        for k in range(half):
            at = i * half + k
            chain_odd[at + 1] = chain_odd[idx_s[0, at]] + dot(mask_t[i, 2 * k + 1], q)
        return carry

    lax.fori_loop(0, blocks, backward_received, 0, unroll=UNROLL)
    returns = [to_dom(t, grad_out, returned, back_send, back_recv, -offsets[t]) for t in range(turns)]
    for t in reversed(range(turns)):
        for i in range(panel):
            grad_out[t * panel + i] = chain_odd[idx_s[1, t * panel + i]].astype(BF16)
        if t not in LATE:
            returns[t].start()

    def backward(i, carry):
        q = q_b[i]
        for k in range(half):
            at = i * half + k
            chain_even[at + 1] = chain_even[idx_s[2, at]] + dot(mask_t[i, 2 * k], q)
        gf[i] = lax.dot_general(dz_b[i], w_self[...], CONTRACT_LANES, preferred_element_type=F32)
        return carry

    lax.fori_loop(0, blocks, backward, 0)

    receive_all(stage_1, ways)
    summed = r1_out[piece].astype(F32)
    for m in range(1, ways):
        summed = summed + r1_in[m - 1].astype(F32)
    bias_high = summed[half_rows : half_rows + bias_rows]
    for j in range(ranks):
        r2_out[j, 0:rows_each] = summed[j * rows_each : (j + 1) * rows_each]
        r2_out[j, rows_each : rows_each + bias_rows] = bias_high
    start_all(stage_2, ranks)
    for t in LATE:
        returns[t].start()
    receive_all(stage_2, ranks)
    summed = r2_out[rank]
    for k in range(1, ranks):
        summed = summed + r2_in[k - 1]
    r3_out[...] = summed
    start_all(stage_3, layers)

    def take(t):
        returns[t].wait_recv()
        for i in range(panel):
            at = t * panel + i
            chain_back[at + 1] = chain_back[idx_s[4, at]] + returned[at].astype(F32)

    order = list(range(turns))
    for t in order[:4]:
        take(t)
    receive_all(stage_3, layers)
    summed = r3_out[...]
    for k in range(1, layers):
        summed = summed + r3_in[k - 1]
    r4[rank] = summed[0:rows_each]
    final_bias = summed[rows_each : rows_each + bias_rows]
    start_all(stage_4, ranks)
    for t in order[4:]:
        take(t)

    right, left, across = (rep + 1) % reps, (rep + 3) % reps, (rep + 2) % reps
    part = blocks // 2

    def owned(block):
        return chain_even[idx_s[3, block]] + chain_back[idx_s[5, block]]

    def to_rep(source, target, at, peer):
        return pltpu.make_async_remote_copy(
            src_ref=source, dst_ref=target, send_sem=x_send.at[at], recv_sem=x_recv.at[at],
            device_id=(dom, peer), device_id_type=MESH,
        )

    passing = [to_rep(x_pass.at[s], got_pass.at[s], s, (right, left)[s]) for s in range(2)]
    for s in range(2):
        for j in range(part):
            x_pass[s, j] = owned(across * blocks + s * part + j).astype(BF16)
        passing[s].start()
    near = [
        [to_rep(x_near.at[s, h], got_near.at[s, h], 2 + 2 * s + h, (right, left)[s]) for h in range(2)]
        for s in range(2)
    ]
    for s in range(2):
        peer = (right, left)[s]
        for j in range(part):
            x_near[s, 0, j] = owned(peer * blocks + (1 - s) * part + j).astype(BF16)
        near[s][0].start()
    for s in range(2):
        peer = (right, left)[s]
        for j in range(part):
            own[s, j] = owned(peer * blocks + s * part + j)
    for s in range(2):
        passing[s].wait_recv()
        for j in range(part):
            x_near[s, 1, j] = (own[s, j] + got_pass[s, j].astype(F32)).astype(BF16)
        near[s][1].start()
    for j in range(blocks):
        own_mine[j] = owned(rep * blocks + j) + gf[j]

    receive_all(stage_4, ranks)
    r5[piece] = r4[...].reshape(half_rows, 128).astype(BF16)
    start_all(stage_5, ways)

    for s in range(2):
        near[s][0].wait_recv()
    for s in range(2):
        near[s][1].wait_recv()
    for s in range(2):
        for j in range(part):
            at = s * part + j
            gf[at] = own_mine[at] + got_near[0, 1 - s, j].astype(F32) + got_near[1, s, j].astype(F32)
    gf_copy = pltpu.make_async_copy(gf, gf_hbm, out_sem.at[1])
    gf_copy.start()

    scale = 1.0 / math.sqrt(nodes)
    receive_all(stage_5, ways)
    for c in range(2):
        columns = slice(c * 128, (c + 1) * 128)
        for h in range(2):
            rows = slice(h * half_rows, (h + 1) * half_rows)
            gs_ref[rows, columns] = r5[c * 2 + h].astype(F32) * scale
            gn_ref[rows, columns] = r5[(2 + c) * 2 + h].astype(F32) * scale
        gb_ref[:, columns] = (final_bias[c : c + 1] + final_bias[2 + c : 3 + c]) * scale

    for send in shared + sends + returns:
        send.wait_send()
    for n in range(len(far)):
        for k in range(1, reps):
            hand_on(n, k).wait_send()
    for s in range(2):
        passing[s].wait_send()
        for h in range(2):
            near[s][h].wait_send()
    finish_all(stage_1, ways)
    finish_all(stage_2, ranks)
    finish_all(stage_3, layers)
    finish_all(stage_4, ranks)
    finish_all(stage_5, ways)
    act_copy.wait()
    gf_copy.wait()


def write_out(*refs):
    count = (len(refs) - 1) // 3
    given, results, held, sem = refs[:count], refs[count : 2 * count], refs[2 * count : 3 * count], refs[-1]
    reads = [pltpu.make_async_copy(given[i], held[i], sem.at[0, i]) for i in range(count)]
    writes = [pltpu.make_async_copy(held[i], results[i], sem.at[1, i]) for i in range(count)]
    for read in reads:
        read.start()
    for read, write in zip(reads, writes):
        read.wait()
        write.start()
    for write in writes:
        write.wait()


def per_device(sizes, features, w_self, w_neigh, bias, cotangent, slot_source, tile_masks, panel_blocks):
    doms, reps, subs, offsets, nodes = sizes
    layers = doms // subs
    blocks, slots, tile, _ = tile_masks.shape
    width, hidden = w_self.shape
    part_blocks = features.shape[0] // tile
    turns, panel = panel_blocks.shape[1:]
    tiles = blocks * slots // 2
    ways, ranks, half_rows = 2 * reps, subs // 2, width // 2
    rows_each = half_rows // ranks
    part = blocks // 2
    dma = pltpu.SemaphoreType.DMA
    any_space = pl.BlockSpec(memory_space=pl.ANY)
    vmem = pl.BlockSpec(memory_space=pltpu.VMEM)
    smem = pl.BlockSpec(memory_space=pltpu.SMEM)
    block = (tile, width)
    scratch = [
        pltpu.VMEM((part_blocks,) + block, BF16),
        pltpu.VMEM((width, hidden), BF16),
        pltpu.VMEM((width, hidden), BF16),
        pltpu.VMEM((1, hidden), F32),
        pltpu.VMEM((blocks, tile, hidden), BF16),
        pltpu.VMEM((blocks, slots, tile, tile), jnp.int32),
        pltpu.VMEM((blocks, slots, tile, tile), BF16),
        pltpu.VMEM((blocks, slots, tile, tile), BF16),
        pltpu.VMEM((blocks,) + block, F32),
        pltpu.VMEM((blocks, tile, hidden), F32),
        pltpu.VMEM((blocks,) + block, F32),
        pltpu.VMEM((width, blocks * tile), BF16),
        pltpu.VMEM((width, blocks * tile), BF16),
        pltpu.VMEM((blocks, tile, hidden), BF16),
        pltpu.VMEM((blocks,) + block, BF16),
        pltpu.VMEM((blocks, tile, hidden), BF16),
        pltpu.VMEM((blocks,) + block, F32),
        pltpu.VMEM((turns * panel,) + block, BF16),
        pltpu.VMEM((turns * panel,) + block, BF16),
        pltpu.VMEM((turns * panel,) + block, BF16),
        pltpu.VMEM((turns * panel,) + block, BF16),
        pltpu.VMEM((tiles + 1,) + block, F32),
        pltpu.VMEM((tiles + 1,) + block, F32),
        pltpu.VMEM((turns * panel + 1,) + block, F32),
        pltpu.VMEM((2, part) + block, F32),
        pltpu.VMEM((blocks,) + block, F32),
        pltpu.VMEM((2, part) + block, BF16),
        pltpu.VMEM((2, 2, part) + block, BF16),
        pltpu.VMEM((2, part) + block, BF16),
        pltpu.VMEM((2, 2, part) + block, BF16),
        pltpu.VMEM((8, 128), jnp.int32),
        pltpu.SMEM((8, 128), jnp.int32),
        pltpu.VMEM((ways, half_rows + 16, 128), BF16),
        pltpu.VMEM((ways - 1, half_rows + 16, 128), BF16),
        pltpu.VMEM((ranks, rows_each + 8, 128), F32),
        pltpu.VMEM((ranks - 1, rows_each + 8, 128), F32),
        pltpu.VMEM((rows_each + 8, 128), F32),
        pltpu.VMEM((layers - 1, rows_each + 8, 128), F32),
        pltpu.VMEM((ranks, rows_each, 128), F32),
        pltpu.VMEM((ways, half_rows, 128), BF16),
        dma((5,)), dma((blocks,)), dma, dma((2,)),
        dma((turns,)), dma((turns,)), dma((2,)), dma((2,)), dma((2 * reps - 2,)), dma((2 * reps - 2,)),
        dma((turns,)), dma((turns,)), dma((6,)), dma((6,)),
        dma((ways - 1,)), dma((ways - 1,)), dma((ranks - 1,)), dma((ranks - 1,)),
        dma((layers - 1,)), dma((layers - 1,)), dma((ranks - 1,)), dma((ranks - 1,)),
        dma((ways - 1,)), dma((ways - 1,)),
    ]
    results = pl.pallas_call(
        functools.partial(kernel, sizes),
        out_shape=(
            jax.ShapeDtypeStruct((blocks, tile, hidden), BF16),
            jax.ShapeDtypeStruct((blocks,) + block, F32),
            jax.ShapeDtypeStruct((width, hidden), F32),
            jax.ShapeDtypeStruct((width, hidden), F32),
            jax.ShapeDtypeStruct((1, hidden), F32),
        ),
        in_specs=[any_space] * 6 + [smem] * 2,
        out_specs=(any_space, any_space, vmem, vmem, vmem),
        scratch_shapes=scratch,
        compiler_params=pltpu.CompilerParams(
            collective_id=0, has_side_effects=True, vmem_limit_bytes=63 * 1024 * 1024
        ),
    )(
        features.reshape((part_blocks,) + block),
        w_self,
        w_neigh,
        bias.reshape(1, hidden),
        cotangent.reshape(blocks, tile, hidden),
        tile_masks,
        slot_source,
        panel_blocks.transpose(1, 0, 2),
    )
    act, gf, gs, gn, gb = pl.pallas_call(
        write_out,
        out_shape=tuple(jax.ShapeDtypeStruct(x.shape, x.dtype) for x in results),
        in_specs=[any_space] * len(results),
        out_specs=(any_space,) * len(results),
        scratch_shapes=[pltpu.VMEM(x.shape, x.dtype) for x in results] + [dma((2, len(results)))],
        compiler_params=pltpu.CompilerParams(vmem_limit_bytes=63 * 1024 * 1024),
    )(*results)
    return (
        act.reshape(blocks * tile, hidden),
        gf.reshape(blocks * tile, width),
        gs,
        gn,
        gb.reshape(hidden),
    )


def solution(mesh):
    doms, reps = mesh.shape["dom"], mesh.shape["rep"]
    subs = 16 if doms % 16 == 0 else doms // 2
    offsets = (1, -1, 2, -2, 3, -3)
    in_specs = (
        P("dom", None),
        P(),
        P(),
        P(),
        P(("dom", "rep"), None),
        P(("dom", "rep"), None),
        P(("dom", "rep"), None, None, None),
        P("dom", None, None),
    )
    out_specs = (P(("dom", "rep"), None), P(("dom", "rep"), None), P(), P(), P())

    def step(features, *rest):
        nodes = features.shape[0] * doms
        return per_device((doms, reps, subs, offsets, nodes), features, *rest)

    return jax.shard_map(step, mesh=mesh, in_specs=in_specs, out_specs=out_specs, check_vma=False)
```

```python
import functools
import math

import jax
import jax.numpy as jnp
from jax import lax
from jax.experimental import pallas as pl
from jax.experimental.pallas import tpu as pltpu
from jax.sharding import PartitionSpec as P

LATE = (4, 5)
UNROLL = 2
MESH = pl.DeviceIdType.MESH
F32 = jnp.float32
BF16 = jnp.bfloat16
CONTRACT_ROWS = (((0,), (0,)), ((), ()))
CONTRACT_LANES = (((1,), (1,)), ((), ()))


def dot(a, b):
    return jnp.dot(a, b, preferred_element_type=F32)


def chain(values):
    lane = lax.broadcasted_iota(jnp.int32, (1, 128), 1)
    listed = jnp.full((1, 128), -1, jnp.int32)
    for j, value in enumerate(values):
        listed = jnp.where(lane == j, value, listed)
    prev = jnp.zeros((1, 128), jnp.int32)
    last = jnp.zeros((1, 128), jnp.int32)
    for i, value in enumerate(values):
        prev = jnp.where((listed == value) & (lane > i), i + 1, prev)
        last = jnp.where(lane == value, i + 1, last)
    return prev, last


def kernel(
    sizes, feat_hbm, w_self_hbm, w_neigh_hbm, bias_hbm, cot_hbm, masks_hbm, slot_ref, panel_ref,
    act_hbm, gf_hbm, gs_ref, gn_ref, gb_ref,
    feat, w_self, w_neigh, bias, cot, masks, mask_b, mask_t, inv, z0, agg_even, feat_t, agg_t, dz_b, q_b, act, gf,
    far_in, far_out, panel_out, recv, grad_out, returned, chain_odd, chain_even, chain_back, own, own_mine, x_pass, x_near,
    got_pass, got_near, idx_v, idx_s,
    r1_out, r1_in, r2_out, r2_in, r3_out, r3_in, r4, r5,
    in_sem, mask_sem, idx_sem, out_sem, fwd_send, fwd_recv, far_send, far_recv, hand_send, hand_recv, gather_send, gather_recv, back_far_send, back_far_recv, back_send, back_recv, x_send, x_recv,
    s1_send, s1_recv, s2_send, s2_recv, s3_send, s3_recv, s4_send, s4_recv, s5_send, s5_recv,
):
    doms, reps, subs, offsets, nodes = sizes
    layers = doms // subs
    turns = len(offsets)
    panel = panel_ref.shape[2]
    blocks, slots = slot_ref.shape
    half = slots // 2
    part_blocks, tile, width = feat.shape
    hidden = w_self.shape[1]
    ways = 2 * reps
    ranks = subs // 2
    half_rows = width // 2
    rows_each = half_rows // ranks
    dom = lax.axis_index("dom")
    rep = lax.axis_index("rep")
    layer = dom // subs
    sub = dom % subs
    rank = sub // 2
    core = dom % 2
    other = 1 - 2 * core
    piece = rep * 2 + core

    def received(i, k):
        return jnp.maximum(slot_ref[i, 2 * k + 1] - part_blocks, 0)

    def columns_of(i):
        return pl.ds(pl.multiple_of(i * tile, tile), tile)

    far = [t for t in range(turns) if abs(offsets[t]) == 3]
    common = panel - reps
    for t in far:
        for i in range(common, panel):
            returned[t * panel + i] = jnp.zeros((tile, width), BF16)

    loads = [
        pltpu.make_async_copy(feat_hbm, feat, in_sem.at[0]),
        pltpu.make_async_copy(w_self_hbm, w_self, in_sem.at[1]),
        pltpu.make_async_copy(w_neigh_hbm, w_neigh, in_sem.at[2]),
        pltpu.make_async_copy(bias_hbm, bias, in_sem.at[3]),
        pltpu.make_async_copy(cot_hbm, cot, in_sem.at[4]),
    ]
    for load in loads:
        load.start()
    for i in range(blocks):
        pltpu.make_async_copy(masks_hbm.at[i], masks.at[i], mask_sem.at[i]).start()

    barrier = pltpu.get_barrier_semaphore()

    def greet(d, r):
        pl.semaphore_signal(barrier, inc=1, device_id=(d, r), device_id_type=MESH)

    for offset in offsets:
        greet((dom + offset + doms) % doms, rep)
    for m in range(1, ways):
        greet(dom + other * (m // reps), (rep + m) % reps)
    for k in range(1, ranks):
        greet(layer * subs + ((rank + k) % ranks) * 2 + core, rep)
    for k in range(1, layers):
        greet(((layer + k) % layers) * subs + sub, rep)

    loads[0].wait()
    for t in range(turns):
        for i in range(panel):
            panel_out[t * panel + i] = feat[panel_ref[t, 0, i]]
    pl.semaphore_wait(barrier, turns + ways - 1 + ranks - 1 + layers - 1)

    def to_dom(t, source, target, send, recv_sem, offset, count=panel):
        part = pl.ds(t * panel, count)
        return pltpu.make_async_remote_copy(
            src_ref=source.at[part], dst_ref=target.at[part], send_sem=send.at[t], recv_sem=recv_sem.at[t],
            device_id=((dom + offset + doms) % doms, rep), device_id_type=MESH,
        )

    def to_far(n, source, target, send, recv_sem, way):
        mine = far[n] * panel + common + rep
        return pltpu.make_async_remote_copy(
            src_ref=source.at[mine], dst_ref=target.at[mine], send_sem=send.at[n], recv_sem=recv_sem.at[n],
            device_id=((dom + way * offsets[far[n]] + doms) % doms, rep), device_id_type=MESH,
        )

    def hand_on(n, k):
        mine = far[n] * panel + common + rep
        at = n * (reps - 1) + k - 1
        return pltpu.make_async_remote_copy(
            src_ref=recv.at[mine], dst_ref=recv.at[mine], send_sem=hand_send.at[at], recv_sem=hand_recv.at[at],
            device_id=(dom, (rep + k) % reps), device_id_type=MESH,
        )

    shared = [to_far(n, panel_out, recv, far_send, far_recv, 1) for n in range(len(far))]
    sends = [
        to_dom(t, panel_out, recv, fwd_send, fwd_recv, offsets[t], common if t in far else panel) for t in range(turns)
    ]
    for send in shared:
        send.start()
    for t in reversed(range(turns)):
        sends[t].start()
    odd = [received(i, k) for i in range(blocks) for k in range(half)]
    even = [slot_ref[i, 2 * k] for i in range(blocks) for k in range(half)]
    back = [panel_ref[t, 0, i] for t in range(turns) for i in range(panel)]
    for at, values in enumerate((odd, even, back)):
        prev, last = chain(values)
        idx_v[2 * at : 2 * at + 1, :] = prev
        idx_v[2 * at + 1 : 2 * at + 2, :] = last
    idx_v[6:8, :] = jnp.zeros((2, 128), jnp.int32)
    idx_copy = pltpu.make_async_copy(idx_v, idx_s, idx_sem)
    idx_copy.start()
    chain_odd[0] = jnp.zeros((tile, width), F32)
    chain_even[0] = jnp.zeros((tile, width), F32)
    chain_back[0] = jnp.zeros((tile, width), F32)
    for n in range(len(far)):
        shared[n].wait_recv()
        for k in range(1, reps):
            hand_on(n, k).start()

    loads[1].wait()
    loads[2].wait()
    loads[3].wait()

    def prepare(i, carry):
        pltpu.make_async_copy(masks_hbm.at[i], masks.at[i], mask_sem.at[i]).wait()
        total = jnp.zeros((tile, tile), F32)
        aggregate = jnp.zeros((tile, width), F32)
        for k in range(slots):
            mask = masks[i, k].astype(F32)
            total = total + mask
            mask = mask.astype(BF16)
            mask_b[i, k] = mask
            mask_t[i, k] = mask.T
            if k % 2 == 0:
                aggregate = aggregate + dot(mask, feat[slot_ref[i, k]])
        agg_even[i] = aggregate
        degree = jnp.maximum(jnp.sum(total, axis=1, keepdims=True), 1.0)
        inv[i] = jnp.broadcast_to(1.0 / degree, (tile, width))
        mine = feat[rep * blocks + i]
        feat_t[:, columns_of(i)] = mine.T
        z0[i] = dot(mine, w_self[...]) + bias[...]
        return carry

    lax.fori_loop(0, blocks, prepare, 0, unroll=UNROLL)
    loads[4].wait()
    idx_copy.wait()
    for send in sends:
        send.wait_recv()
    for n in range(len(far)):
        for k in range(1, reps):
            hand_on(n, k).wait_recv()

    def forward(i, bias_total):
        aggregate = agg_even[i]
        for k in range(half):
            aggregate = aggregate + dot(mask_b[i, 2 * k + 1], recv[received(i, k)])
        agg = (aggregate * inv[i]).astype(BF16)
        agg_t[:, columns_of(i)] = agg.T
        z = z0[i] + dot(agg, w_neigh[...])
        sig = lax.logistic(z)
        act[i] = (z * sig).astype(BF16)
        dz = cot[i].astype(F32) * (sig * (1.0 + z * (1.0 - sig)))
        dzb = dz.astype(BF16)
        dz_b[i] = dzb
        q = lax.dot_general(dzb, w_neigh[...], CONTRACT_LANES, preferred_element_type=F32)
        q = (q * inv[i]).astype(BF16)
        q_b[i] = q
        return bias_total + jnp.sum(dz, axis=0, keepdims=True)

    bias_total = lax.fori_loop(0, blocks, forward, jnp.zeros((1, hidden), F32), unroll=UNROLL)
    act_copy = pltpu.make_async_copy(act, act_hbm, out_sem.at[0])
    act_copy.start()

    bias_rows = 8
    packed_rows = 16
    dz_all = dz_b[...].reshape(blocks * tile, hidden)
    row = lax.broadcasted_iota(jnp.int32, (packed_rows, 128), 0)
    bias_high = bias_total.astype(BF16).astype(F32)
    bias_low = bias_total - bias_high
    bias_tile = jnp.zeros((packed_rows, 128), F32)
    for at, line in enumerate((bias_high, bias_low)):
        for c in range(2):
            bias_tile = jnp.where(row == 2 * at + c, line[:, c * 128 : (c + 1) * 128], bias_tile)
    bias_tile = bias_tile.astype(BF16)
    for at, left_side in enumerate((feat_t, agg_t)):
        part = dot(left_side[...], dz_all).astype(BF16)
        for c in range(2):
            for h in range(2):
                to = (2 * at + c) * 2 + h
                r1_out[to, 0:half_rows] = part[h * half_rows : (h + 1) * half_rows, c * 128 : (c + 1) * 128]
                r1_out[to, half_rows : half_rows + packed_rows] = bias_tile

    def near_by(m):
        return dom + other * (m // reps), (rep + m) % reps

    def stage_1(m):
        peer, peer_rep = near_by(m)
        return pltpu.make_async_remote_copy(
            src_ref=r1_out.at[peer_rep * 2 + peer % 2], dst_ref=r1_in.at[m - 1],
            send_sem=s1_send.at[m - 1], recv_sem=s1_recv.at[m - 1],
            device_id=(peer, peer_rep), device_id_type=MESH,
        )

    def stage_2(k):
        peer = (rank + k) % ranks
        return pltpu.make_async_remote_copy(
            src_ref=r2_out.at[peer], dst_ref=r2_in.at[k - 1], send_sem=s2_send.at[k - 1], recv_sem=s2_recv.at[k - 1],
            device_id=(layer * subs + peer * 2 + core, rep), device_id_type=MESH,
        )

    def stage_3(k):
        peer = (layer + k) % layers
        return pltpu.make_async_remote_copy(
            src_ref=r3_out, dst_ref=r3_in.at[k - 1], send_sem=s3_send.at[k - 1], recv_sem=s3_recv.at[k - 1],
            device_id=(peer * subs + sub, rep), device_id_type=MESH,
        )

    def stage_4(k):
        peer = (rank + k) % ranks
        return pltpu.make_async_remote_copy(
            src_ref=r4.at[rank], dst_ref=r4.at[rank], send_sem=s4_send.at[k - 1], recv_sem=s4_recv.at[k - 1],
            device_id=(layer * subs + peer * 2 + core, rep), device_id_type=MESH,
        )

    def stage_5(m):
        peer, peer_rep = near_by(m)
        return pltpu.make_async_remote_copy(
            src_ref=r5.at[piece], dst_ref=r5.at[piece], send_sem=s5_send.at[m - 1], recv_sem=s5_recv.at[m - 1],
            device_id=(peer, peer_rep), device_id_type=MESH,
        )

    def start_all(stage, count):
        for k in range(1, count):
            stage(k).start()

    def receive_all(stage, count):
        for k in range(1, count):
            stage(k).wait_recv()

    def finish_all(stage, count):
        for k in range(1, count):
            stage(k).wait_send()

    start_all(stage_1, ways)

    def backward_received(i, carry):
        q = q_b[i]
        for k in range(half):
            at = i * half + k
            chain_odd[at + 1] = chain_odd[idx_s[0, at]] + dot(mask_t[i, 2 * k + 1], q)
        return carry

    lax.fori_loop(0, blocks, backward_received, 0, unroll=UNROLL)
    returns = [
        to_dom(t, grad_out, returned, back_send, back_recv, -offsets[t], common if t in far else panel)
        for t in range(turns)
    ]

    def gather_far(n, k):
        peer = (rep + k) % reps
        at = n * (reps - 1) + k - 1
        return pltpu.make_async_remote_copy(
            src_ref=grad_out.at[far[n] * panel + common + peer], dst_ref=far_in.at[at],
            send_sem=gather_send.at[at], recv_sem=gather_recv.at[at], device_id=(dom, peer), device_id_type=MESH,
        )

    def return_far(n):
        return pltpu.make_async_remote_copy(
            src_ref=far_out.at[n], dst_ref=returned.at[far[n] * panel + common + rep],
            send_sem=back_far_send.at[n], recv_sem=back_far_recv.at[n],
            device_id=((dom - offsets[far[n]] + doms) % doms, rep), device_id_type=MESH,
        )

    for t in reversed(range(turns)):
        for i in range(panel):
            grad_out[t * panel + i] = chain_odd[idx_s[1, t * panel + i]].astype(BF16)
        if t in far:
            for k in range(1, reps):
                gather_far(far.index(t), k).start()
        if t not in LATE:
            returns[t].start()

    def backward(i, carry):
        q = q_b[i]
        for k in range(half):
            at = i * half + k
            chain_even[at + 1] = chain_even[idx_s[2, at]] + dot(mask_t[i, 2 * k], q)
        gf[i] = lax.dot_general(dz_b[i], w_self[...], CONTRACT_LANES, preferred_element_type=F32)
        return carry

    lax.fori_loop(0, blocks, backward, 0)

    receive_all(stage_1, ways)
    summed = r1_out[piece].astype(F32)
    for m in range(1, ways):
        summed = summed + r1_in[m - 1].astype(F32)
    bias_high = summed[half_rows : half_rows + bias_rows]
    for j in range(ranks):
        r2_out[j, 0:rows_each] = summed[j * rows_each : (j + 1) * rows_each]
        r2_out[j, rows_each : rows_each + bias_rows] = bias_high
    start_all(stage_2, ranks)
    for n in range(len(far)):
        total = grad_out[far[n] * panel + common + rep].astype(F32)
        for k in range(1, reps):
            gather_far(n, k).wait_recv()
            total = total + far_in[n * (reps - 1) + k - 1].astype(F32)
        far_out[n] = total.astype(BF16)
        return_far(n).start()
    for t in LATE:
        returns[t].start()
    receive_all(stage_2, ranks)
    summed = r2_out[rank]
    for k in range(1, ranks):
        summed = summed + r2_in[k - 1]
    r3_out[...] = summed
    start_all(stage_3, layers)

    def take(t):
        returns[t].wait_recv()
        if t in far:
            return_far(far.index(t)).wait_recv()
        for i in range(panel):
            at = t * panel + i
            chain_back[at + 1] = chain_back[idx_s[4, at]] + returned[at].astype(F32)

    order = list(range(turns))
    for t in order[:4]:
        take(t)
    receive_all(stage_3, layers)
    summed = r3_out[...]
    for k in range(1, layers):
        summed = summed + r3_in[k - 1]
    r4[rank] = summed[0:rows_each]
    final_bias = summed[rows_each : rows_each + bias_rows]
    start_all(stage_4, ranks)
    for t in order[4:]:
        take(t)

    right, left, across = (rep + 1) % reps, (rep + 3) % reps, (rep + 2) % reps
    part = blocks // 2

    def owned(block):
        return chain_even[idx_s[3, block]] + chain_back[idx_s[5, block]]

    def to_rep(source, target, at, peer):
        return pltpu.make_async_remote_copy(
            src_ref=source, dst_ref=target, send_sem=x_send.at[at], recv_sem=x_recv.at[at],
            device_id=(dom, peer), device_id_type=MESH,
        )

    passing = [to_rep(x_pass.at[s], got_pass.at[s], s, (right, left)[s]) for s in range(2)]
    for s in range(2):
        for j in range(part):
            x_pass[s, j] = owned(across * blocks + s * part + j).astype(BF16)
        passing[s].start()
    near = [
        [to_rep(x_near.at[s, h], got_near.at[s, h], 2 + 2 * s + h, (right, left)[s]) for h in range(2)]
        for s in range(2)
    ]
    for s in range(2):
        peer = (right, left)[s]
        for j in range(part):
            x_near[s, 0, j] = owned(peer * blocks + (1 - s) * part + j).astype(BF16)
        near[s][0].start()
    for s in range(2):
        peer = (right, left)[s]
        for j in range(part):
            own[s, j] = owned(peer * blocks + s * part + j)
    for s in range(2):
        passing[s].wait_recv()
        for j in range(part):
            x_near[s, 1, j] = (own[s, j] + got_pass[s, j].astype(F32)).astype(BF16)
        near[s][1].start()
    for j in range(blocks):
        own_mine[j] = owned(rep * blocks + j) + gf[j]

    receive_all(stage_4, ranks)
    r5[piece] = r4[...].reshape(half_rows, 128).astype(BF16)
    start_all(stage_5, ways)

    for s in range(2):
        near[s][0].wait_recv()
    for s in range(2):
        near[s][1].wait_recv()
    for s in range(2):
        for j in range(part):
            at = s * part + j
            gf[at] = own_mine[at] + got_near[0, 1 - s, j].astype(F32) + got_near[1, s, j].astype(F32)
    gf_copy = pltpu.make_async_copy(gf, gf_hbm, out_sem.at[1])
    gf_copy.start()

    scale = 1.0 / math.sqrt(nodes)
    receive_all(stage_5, ways)
    for c in range(2):
        columns = slice(c * 128, (c + 1) * 128)
        for h in range(2):
            rows = slice(h * half_rows, (h + 1) * half_rows)
            gs_ref[rows, columns] = r5[c * 2 + h].astype(F32) * scale
            gn_ref[rows, columns] = r5[(2 + c) * 2 + h].astype(F32) * scale
        gb_ref[:, columns] = (final_bias[c : c + 1] + final_bias[2 + c : 3 + c]) * scale

    for send in shared + sends + returns:
        send.wait_send()
    for n in range(len(far)):
        for k in range(1, reps):
            hand_on(n, k).wait_send()
            gather_far(n, k).wait_send()
        return_far(n).wait_send()
    for s in range(2):
        passing[s].wait_send()
        for h in range(2):
            near[s][h].wait_send()
    finish_all(stage_1, ways)
    finish_all(stage_2, ranks)
    finish_all(stage_3, layers)
    finish_all(stage_4, ranks)
    finish_all(stage_5, ways)
    act_copy.wait()
    gf_copy.wait()


def write_out(*refs):
    count = (len(refs) - 1) // 3
    given, results, held, sem = refs[:count], refs[count : 2 * count], refs[2 * count : 3 * count], refs[-1]
    reads = [pltpu.make_async_copy(given[i], held[i], sem.at[0, i]) for i in range(count)]
    writes = [pltpu.make_async_copy(held[i], results[i], sem.at[1, i]) for i in range(count)]
    for read in reads:
        read.start()
    for read, write in zip(reads, writes):
        read.wait()
        write.start()
    for write in writes:
        write.wait()


def per_device(sizes, features, w_self, w_neigh, bias, cotangent, slot_source, tile_masks, panel_blocks):
    doms, reps, subs, offsets, nodes = sizes
    layers = doms // subs
    blocks, slots, tile, _ = tile_masks.shape
    width, hidden = w_self.shape
    part_blocks = features.shape[0] // tile
    turns, panel = panel_blocks.shape[1:]
    tiles = blocks * slots // 2
    ways, ranks, half_rows = 2 * reps, subs // 2, width // 2
    rows_each = half_rows // ranks
    part = blocks // 2
    dma = pltpu.SemaphoreType.DMA
    any_space = pl.BlockSpec(memory_space=pl.ANY)
    vmem = pl.BlockSpec(memory_space=pltpu.VMEM)
    smem = pl.BlockSpec(memory_space=pltpu.SMEM)
    block = (tile, width)
    scratch = [
        pltpu.VMEM((part_blocks,) + block, BF16),
        pltpu.VMEM((width, hidden), BF16),
        pltpu.VMEM((width, hidden), BF16),
        pltpu.VMEM((1, hidden), F32),
        pltpu.VMEM((blocks, tile, hidden), BF16),
        pltpu.VMEM((blocks, slots, tile, tile), jnp.int32),
        pltpu.VMEM((blocks, slots, tile, tile), BF16),
        pltpu.VMEM((blocks, slots, tile, tile), BF16),
        pltpu.VMEM((blocks,) + block, F32),
        pltpu.VMEM((blocks, tile, hidden), F32),
        pltpu.VMEM((blocks,) + block, F32),
        pltpu.VMEM((width, blocks * tile), BF16),
        pltpu.VMEM((width, blocks * tile), BF16),
        pltpu.VMEM((blocks, tile, hidden), BF16),
        pltpu.VMEM((blocks,) + block, BF16),
        pltpu.VMEM((blocks, tile, hidden), BF16),
        pltpu.VMEM((blocks,) + block, F32),
        pltpu.VMEM((2 * reps - 2,) + block, BF16),
        pltpu.VMEM((2,) + block, BF16),
        pltpu.VMEM((turns * panel,) + block, BF16),
        pltpu.VMEM((turns * panel,) + block, BF16),
        pltpu.VMEM((turns * panel,) + block, BF16),
        pltpu.VMEM((turns * panel,) + block, BF16),
        pltpu.VMEM((tiles + 1,) + block, F32),
        pltpu.VMEM((tiles + 1,) + block, F32),
        pltpu.VMEM((turns * panel + 1,) + block, F32),
        pltpu.VMEM((2, part) + block, F32),
        pltpu.VMEM((blocks,) + block, F32),
        pltpu.VMEM((2, part) + block, BF16),
        pltpu.VMEM((2, 2, part) + block, BF16),
        pltpu.VMEM((2, part) + block, BF16),
        pltpu.VMEM((2, 2, part) + block, BF16),
        pltpu.VMEM((8, 128), jnp.int32),
        pltpu.SMEM((8, 128), jnp.int32),
        pltpu.VMEM((ways, half_rows + 16, 128), BF16),
        pltpu.VMEM((ways - 1, half_rows + 16, 128), BF16),
        pltpu.VMEM((ranks, rows_each + 8, 128), F32),
        pltpu.VMEM((ranks - 1, rows_each + 8, 128), F32),
        pltpu.VMEM((rows_each + 8, 128), F32),
        pltpu.VMEM((layers - 1, rows_each + 8, 128), F32),
        pltpu.VMEM((ranks, rows_each, 128), F32),
        pltpu.VMEM((ways, half_rows, 128), BF16),
        dma((5,)), dma((blocks,)), dma, dma((2,)),
        dma((turns,)), dma((turns,)), dma((2,)), dma((2,)), dma((2 * reps - 2,)), dma((2 * reps - 2,)),
        dma((2 * reps - 2,)), dma((2 * reps - 2,)), dma((2,)), dma((2,)),
        dma((turns,)), dma((turns,)), dma((6,)), dma((6,)),
        dma((ways - 1,)), dma((ways - 1,)), dma((ranks - 1,)), dma((ranks - 1,)),
        dma((layers - 1,)), dma((layers - 1,)), dma((ranks - 1,)), dma((ranks - 1,)),
        dma((ways - 1,)), dma((ways - 1,)),
    ]
    results = pl.pallas_call(
        functools.partial(kernel, sizes),
        out_shape=(
            jax.ShapeDtypeStruct((blocks, tile, hidden), BF16),
            jax.ShapeDtypeStruct((blocks,) + block, F32),
            jax.ShapeDtypeStruct((width, hidden), F32),
            jax.ShapeDtypeStruct((width, hidden), F32),
            jax.ShapeDtypeStruct((1, hidden), F32),
        ),
        in_specs=[any_space] * 6 + [smem] * 2,
        out_specs=(any_space, any_space, vmem, vmem, vmem),
        scratch_shapes=scratch,
        compiler_params=pltpu.CompilerParams(
            collective_id=0, has_side_effects=True, vmem_limit_bytes=63 * 1024 * 1024
        ),
    )(
        features.reshape((part_blocks,) + block),
        w_self,
        w_neigh,
        bias.reshape(1, hidden),
        cotangent.reshape(blocks, tile, hidden),
        tile_masks,
        slot_source,
        panel_blocks.transpose(1, 0, 2),
    )
    act, gf, gs, gn, gb = pl.pallas_call(
        write_out,
        out_shape=tuple(jax.ShapeDtypeStruct(x.shape, x.dtype) for x in results),
        in_specs=[any_space] * len(results),
        out_specs=(any_space,) * len(results),
        scratch_shapes=[pltpu.VMEM(x.shape, x.dtype) for x in results] + [dma((2, len(results)))],
        compiler_params=pltpu.CompilerParams(vmem_limit_bytes=63 * 1024 * 1024),
    )(*results)
    return (
        act.reshape(blocks * tile, hidden),
        gf.reshape(blocks * tile, width),
        gs,
        gn,
        gb.reshape(hidden),
    )


def solution(mesh):
    doms, reps = mesh.shape["dom"], mesh.shape["rep"]
    subs = 16 if doms % 16 == 0 else doms // 2
    offsets = (1, -1, 2, -2, 3, -3)
    in_specs = (
        P("dom", None),
        P(),
        P(),
        P(),
        P(("dom", "rep"), None),
        P(("dom", "rep"), None),
        P(("dom", "rep"), None, None, None),
        P("dom", None, None),
    )
    out_specs = (P(("dom", "rep"), None), P(("dom", "rep"), None), P(), P(), P())

    def step(features, *rest):
        nodes = features.shape[0] * doms
        return per_device((doms, reps, subs, offsets, nodes), features, *rest)

    return jax.shard_map(step, mesh=mesh, in_specs=in_specs, out_specs=out_specs, check_vma=False)
```

```python
import functools
import math

import jax
import jax.numpy as jnp
from jax import lax
from jax.experimental import pallas as pl
from jax.experimental.pallas import tpu as pltpu
from jax.sharding import PartitionSpec as P

LATE = (4, 5)
UNROLL = 3
MESH = pl.DeviceIdType.MESH
F32 = jnp.float32
BF16 = jnp.bfloat16
CONTRACT_ROWS = (((0,), (0,)), ((), ()))
CONTRACT_LANES = (((1,), (1,)), ((), ()))


def dot(a, b):
    return jnp.dot(a, b, preferred_element_type=F32)


def chain(values):
    lane = lax.broadcasted_iota(jnp.int32, (1, 128), 1)
    listed = jnp.full((1, 128), -1, jnp.int32)
    for j, value in enumerate(values):
        listed = jnp.where(lane == j, value, listed)
    prev = jnp.zeros((1, 128), jnp.int32)
    last = jnp.zeros((1, 128), jnp.int32)
    for i, value in enumerate(values):
        prev = jnp.where((listed == value) & (lane > i), i + 1, prev)
        last = jnp.where(lane == value, i + 1, last)
    return prev, last


def kernel(
    sizes, feat_hbm, w_self_hbm, w_neigh_hbm, bias_hbm, cot_hbm, masks_hbm, slot_ref, panel_ref,
    act_hbm, gf_hbm, gs_ref, gn_ref, gb_ref,
    feat, w_self, w_neigh, bias, cot, masks, mask_b, mask_t, inv, z0, agg_even, feat_t, agg_t, dz_b, q_b, act, gf,
    far_in, far_out, panel_out, recv, grad_out, returned, chain_odd, chain_even, chain_back, own, own_mine, x_pass, x_near,
    got_pass, got_near, idx_v, idx_s,
    r1_out, r1_in, r2_out, r2_in, r3_out, r3_in, r4, r5,
    in_sem, mask_sem, idx_sem, out_sem, fwd_send, fwd_recv, far_send, far_recv, hand_send, hand_recv, gather_send, gather_recv, back_far_send, back_far_recv, back_send, back_recv, x_send, x_recv,
    s1_send, s1_recv, s2_send, s2_recv, s3_send, s3_recv, s4_send, s4_recv, s5_send, s5_recv,
):
    doms, reps, subs, offsets, nodes = sizes
    layers = doms // subs
    turns = len(offsets)
    panel = panel_ref.shape[2]
    blocks, slots = slot_ref.shape
    half = slots // 2
    part_blocks, tile, width = feat.shape
    hidden = w_self.shape[1]
    ways = 2 * reps
    ranks = subs // 2
    half_rows = width // 2
    rows_each = half_rows // ranks
    dom = lax.axis_index("dom")
    rep = lax.axis_index("rep")
    layer = dom // subs
    sub = dom % subs
    rank = sub // 2
    core = dom % 2
    other = 1 - 2 * core
    piece = rep * 2 + core

    def received(i, k):
        return jnp.maximum(slot_ref[i, 2 * k + 1] - part_blocks, 0)

    def columns_of(i):
        return pl.ds(pl.multiple_of(i * tile, tile), tile)

    far = [t for t in range(turns) if abs(offsets[t]) == 3]
    common = panel - reps
    for t in far:
        for i in range(common, panel):
            returned[t * panel + i] = jnp.zeros((tile, width), BF16)

    loads = [
        pltpu.make_async_copy(feat_hbm, feat, in_sem.at[0]),
        pltpu.make_async_copy(w_self_hbm, w_self, in_sem.at[1]),
        pltpu.make_async_copy(w_neigh_hbm, w_neigh, in_sem.at[2]),
        pltpu.make_async_copy(bias_hbm, bias, in_sem.at[3]),
        pltpu.make_async_copy(cot_hbm, cot, in_sem.at[4]),
    ]
    for load in loads:
        load.start()
    for i in range(blocks):
        pltpu.make_async_copy(masks_hbm.at[i], masks.at[i], mask_sem.at[i]).start()

    barrier = pltpu.get_barrier_semaphore()

    def greet(d, r):
        pl.semaphore_signal(barrier, inc=1, device_id=(d, r), device_id_type=MESH)

    for offset in offsets:
        greet((dom + offset + doms) % doms, rep)
    for m in range(1, ways):
        greet(dom + other * (m // reps), (rep + m) % reps)
    for k in range(1, ranks):
        greet(layer * subs + ((rank + k) % ranks) * 2 + core, rep)
    for k in range(1, layers):
        greet(((layer + k) % layers) * subs + sub, rep)

    loads[0].wait()
    for t in range(turns):
        for i in range(panel):
            panel_out[t * panel + i] = feat[panel_ref[t, 0, i]]
    pl.semaphore_wait(barrier, turns + ways - 1 + ranks - 1 + layers - 1)

    def to_dom(t, source, target, send, recv_sem, offset, count=panel):
        part = pl.ds(t * panel, count)
        return pltpu.make_async_remote_copy(
            src_ref=source.at[part], dst_ref=target.at[part], send_sem=send.at[t], recv_sem=recv_sem.at[t],
            device_id=((dom + offset + doms) % doms, rep), device_id_type=MESH,
        )

    def to_far(n, source, target, send, recv_sem, way):
        mine = far[n] * panel + common + rep
        return pltpu.make_async_remote_copy(
            src_ref=source.at[mine], dst_ref=target.at[mine], send_sem=send.at[n], recv_sem=recv_sem.at[n],
            device_id=((dom + way * offsets[far[n]] + doms) % doms, rep), device_id_type=MESH,
        )

    def hand_on(n, k):
        mine = far[n] * panel + common + rep
        at = n * (reps - 1) + k - 1
        return pltpu.make_async_remote_copy(
            src_ref=recv.at[mine], dst_ref=recv.at[mine], send_sem=hand_send.at[at], recv_sem=hand_recv.at[at],
            device_id=(dom, (rep + k) % reps), device_id_type=MESH,
        )

    shared = [to_far(n, panel_out, recv, far_send, far_recv, 1) for n in range(len(far))]
    sends = [
        to_dom(t, panel_out, recv, fwd_send, fwd_recv, offsets[t], common if t in far else panel) for t in range(turns)
    ]
    for send in shared:
        send.start()
    for t in reversed(range(turns)):
        sends[t].start()
    odd = [received(i, k) for i in range(blocks) for k in range(half)]
    even = [slot_ref[i, 2 * k] for i in range(blocks) for k in range(half)]
    back = [panel_ref[t, 0, i] for t in range(turns) for i in range(panel)]
    for at, values in enumerate((odd, even, back)):
        prev, last = chain(values)
        idx_v[2 * at : 2 * at + 1, :] = prev
        idx_v[2 * at + 1 : 2 * at + 2, :] = last
    idx_v[6:8, :] = jnp.zeros((2, 128), jnp.int32)
    idx_copy = pltpu.make_async_copy(idx_v, idx_s, idx_sem)
    idx_copy.start()
    chain_odd[0] = jnp.zeros((tile, width), F32)
    chain_even[0] = jnp.zeros((tile, width), F32)
    chain_back[0] = jnp.zeros((tile, width), F32)
    for n in range(len(far)):
        shared[n].wait_recv()
        for k in range(1, reps):
            hand_on(n, k).start()

    loads[1].wait()
    loads[2].wait()
    loads[3].wait()

    def prepare(i, carry):
        pltpu.make_async_copy(masks_hbm.at[i], masks.at[i], mask_sem.at[i]).wait()
        total = jnp.zeros((tile, tile), F32)
        aggregate = jnp.zeros((tile, width), F32)
        for k in range(slots):
            mask = masks[i, k].astype(F32)
            total = total + mask
            mask = mask.astype(BF16)
            mask_b[i, k] = mask
            mask_t[i, k] = mask.T
            if k % 2 == 0:
                aggregate = aggregate + dot(mask, feat[slot_ref[i, k]])
        agg_even[i] = aggregate
        degree = jnp.maximum(jnp.sum(total, axis=1, keepdims=True), 1.0)
        inv[i] = jnp.broadcast_to(1.0 / degree, (tile, width))
        mine = feat[rep * blocks + i]
        feat_t[:, columns_of(i)] = mine.T
        z0[i] = dot(mine, w_self[...]) + bias[...]
        return carry

    lax.fori_loop(0, blocks, prepare, 0, unroll=UNROLL)
    loads[4].wait()
    idx_copy.wait()
    for send in sends:
        send.wait_recv()
    for n in range(len(far)):
        for k in range(1, reps):
            hand_on(n, k).wait_recv()

    def forward(i, bias_total):
        aggregate = agg_even[i]
        for k in range(half):
            aggregate = aggregate + dot(mask_b[i, 2 * k + 1], recv[received(i, k)])
        agg = (aggregate * inv[i]).astype(BF16)
        agg_t[:, columns_of(i)] = agg.T
        z = z0[i] + dot(agg, w_neigh[...])
        sig = lax.logistic(z)
        act[i] = (z * sig).astype(BF16)
        dz = cot[i].astype(F32) * (sig * (1.0 + z * (1.0 - sig)))
        dzb = dz.astype(BF16)
        dz_b[i] = dzb
        q = lax.dot_general(dzb, w_neigh[...], CONTRACT_LANES, preferred_element_type=F32)
        q = (q * inv[i]).astype(BF16)
        q_b[i] = q
        return bias_total + jnp.sum(dz, axis=0, keepdims=True)

    bias_total = lax.fori_loop(0, blocks, forward, jnp.zeros((1, hidden), F32), unroll=UNROLL)
    act_copy = pltpu.make_async_copy(act, act_hbm, out_sem.at[0])
    act_copy.start()

    bias_rows = 8
    packed_rows = 16
    dz_all = dz_b[...].reshape(blocks * tile, hidden)
    row = lax.broadcasted_iota(jnp.int32, (packed_rows, 128), 0)
    bias_high = bias_total.astype(BF16).astype(F32)
    bias_low = bias_total - bias_high
    bias_tile = jnp.zeros((packed_rows, 128), F32)
    for at, line in enumerate((bias_high, bias_low)):
        for c in range(2):
            bias_tile = jnp.where(row == 2 * at + c, line[:, c * 128 : (c + 1) * 128], bias_tile)
    bias_tile = bias_tile.astype(BF16)
    for at, left_side in enumerate((feat_t, agg_t)):
        part = dot(left_side[...], dz_all).astype(BF16)
        for c in range(2):
            for h in range(2):
                to = (2 * at + c) * 2 + h
                r1_out[to, 0:half_rows] = part[h * half_rows : (h + 1) * half_rows, c * 128 : (c + 1) * 128]
                r1_out[to, half_rows : half_rows + packed_rows] = bias_tile

    def near_by(m):
        return dom + other * (m // reps), (rep + m) % reps

    def stage_1(m):
        peer, peer_rep = near_by(m)
        return pltpu.make_async_remote_copy(
            src_ref=r1_out.at[peer_rep * 2 + peer % 2], dst_ref=r1_in.at[m - 1],
            send_sem=s1_send.at[m - 1], recv_sem=s1_recv.at[m - 1],
            device_id=(peer, peer_rep), device_id_type=MESH,
        )

    def stage_2(k):
        peer = (rank + k) % ranks
        return pltpu.make_async_remote_copy(
            src_ref=r2_out.at[peer], dst_ref=r2_in.at[k - 1], send_sem=s2_send.at[k - 1], recv_sem=s2_recv.at[k - 1],
            device_id=(layer * subs + peer * 2 + core, rep), device_id_type=MESH,
        )

    def stage_3(k):
        peer = (layer + k) % layers
        return pltpu.make_async_remote_copy(
            src_ref=r3_out, dst_ref=r3_in.at[k - 1], send_sem=s3_send.at[k - 1], recv_sem=s3_recv.at[k - 1],
            device_id=(peer * subs + sub, rep), device_id_type=MESH,
        )

    def stage_4(k):
        peer = (rank + k) % ranks
        return pltpu.make_async_remote_copy(
            src_ref=r4.at[rank], dst_ref=r4.at[rank], send_sem=s4_send.at[k - 1], recv_sem=s4_recv.at[k - 1],
            device_id=(layer * subs + peer * 2 + core, rep), device_id_type=MESH,
        )

    def stage_5(m):
        peer, peer_rep = near_by(m)
        return pltpu.make_async_remote_copy(
            src_ref=r5.at[piece], dst_ref=r5.at[piece], send_sem=s5_send.at[m - 1], recv_sem=s5_recv.at[m - 1],
            device_id=(peer, peer_rep), device_id_type=MESH,
        )

    def start_all(stage, count):
        for k in range(1, count):
            stage(k).start()

    def receive_all(stage, count):
        for k in range(1, count):
            stage(k).wait_recv()

    def finish_all(stage, count):
        for k in range(1, count):
            stage(k).wait_send()

    start_all(stage_1, ways)

    def backward_received(i, carry):
        q = q_b[i]
        for k in range(half):
            at = i * half + k
            chain_odd[at + 1] = chain_odd[idx_s[0, at]] + dot(mask_t[i, 2 * k + 1], q)
        return carry

    lax.fori_loop(0, blocks, backward_received, 0, unroll=UNROLL)
    returns = [
        to_dom(t, grad_out, returned, back_send, back_recv, -offsets[t], common if t in far else panel)
        for t in range(turns)
    ]

    def gather_far(n, k):
        peer = (rep + k) % reps
        at = n * (reps - 1) + k - 1
        return pltpu.make_async_remote_copy(
            src_ref=grad_out.at[far[n] * panel + common + peer], dst_ref=far_in.at[at],
            send_sem=gather_send.at[at], recv_sem=gather_recv.at[at], device_id=(dom, peer), device_id_type=MESH,
        )

    def return_far(n):
        return pltpu.make_async_remote_copy(
            src_ref=far_out.at[n], dst_ref=returned.at[far[n] * panel + common + rep],
            send_sem=back_far_send.at[n], recv_sem=back_far_recv.at[n],
            device_id=((dom - offsets[far[n]] + doms) % doms, rep), device_id_type=MESH,
        )

    for t in reversed(range(turns)):
        for i in range(panel):
            grad_out[t * panel + i] = chain_odd[idx_s[1, t * panel + i]].astype(BF16)
        if t in far:
            for k in range(1, reps):
                gather_far(far.index(t), k).start()
        if t not in LATE:
            returns[t].start()

    def backward(i, carry):
        q = q_b[i]
        for k in range(half):
            at = i * half + k
            chain_even[at + 1] = chain_even[idx_s[2, at]] + dot(mask_t[i, 2 * k], q)
        gf[i] = lax.dot_general(dz_b[i], w_self[...], CONTRACT_LANES, preferred_element_type=F32)
        return carry

    lax.fori_loop(0, blocks, backward, 0)

    receive_all(stage_1, ways)
    summed = r1_out[piece].astype(F32)
    for m in range(1, ways):
        summed = summed + r1_in[m - 1].astype(F32)
    bias_high = summed[half_rows : half_rows + bias_rows]
    for j in range(ranks):
        r2_out[j, 0:rows_each] = summed[j * rows_each : (j + 1) * rows_each]
        r2_out[j, rows_each : rows_each + bias_rows] = bias_high
    start_all(stage_2, ranks)
    for n in range(len(far)):
        total = grad_out[far[n] * panel + common + rep].astype(F32)
        for k in range(1, reps):
            gather_far(n, k).wait_recv()
            total = total + far_in[n * (reps - 1) + k - 1].astype(F32)
        far_out[n] = total.astype(BF16)
        return_far(n).start()
    for t in LATE:
        returns[t].start()
    receive_all(stage_2, ranks)
    summed = r2_out[rank]
    for k in range(1, ranks):
        summed = summed + r2_in[k - 1]
    r3_out[...] = summed
    start_all(stage_3, layers)

    def take(t):
        returns[t].wait_recv()
        if t in far:
            return_far(far.index(t)).wait_recv()
        for i in range(panel):
            at = t * panel + i
            chain_back[at + 1] = chain_back[idx_s[4, at]] + returned[at].astype(F32)

    order = list(range(turns))
    for t in order[:4]:
        take(t)
    receive_all(stage_3, layers)
    summed = r3_out[...]
    for k in range(1, layers):
        summed = summed + r3_in[k - 1]
    r4[rank] = summed[0:rows_each]
    final_bias = summed[rows_each : rows_each + bias_rows]
    start_all(stage_4, ranks)
    for t in order[4:]:
        take(t)

    right, left, across = (rep + 1) % reps, (rep + 3) % reps, (rep + 2) % reps
    part = blocks // 2

    def owned(block):
        return chain_even[idx_s[3, block]] + chain_back[idx_s[5, block]]

    def to_rep(source, target, at, peer):
        return pltpu.make_async_remote_copy(
            src_ref=source, dst_ref=target, send_sem=x_send.at[at], recv_sem=x_recv.at[at],
            device_id=(dom, peer), device_id_type=MESH,
        )

    passing = [to_rep(x_pass.at[s], got_pass.at[s], s, (right, left)[s]) for s in range(2)]
    for s in range(2):
        for j in range(part):
            x_pass[s, j] = owned(across * blocks + s * part + j).astype(BF16)
        passing[s].start()
    near = [
        [to_rep(x_near.at[s, h], got_near.at[s, h], 2 + 2 * s + h, (right, left)[s]) for h in range(2)]
        for s in range(2)
    ]
    for s in range(2):
        peer = (right, left)[s]
        for j in range(part):
            x_near[s, 0, j] = owned(peer * blocks + (1 - s) * part + j).astype(BF16)
        near[s][0].start()
    for s in range(2):
        peer = (right, left)[s]
        for j in range(part):
            own[s, j] = owned(peer * blocks + s * part + j)
    for s in range(2):
        passing[s].wait_recv()
        for j in range(part):
            x_near[s, 1, j] = (own[s, j] + got_pass[s, j].astype(F32)).astype(BF16)
        near[s][1].start()
    for j in range(blocks):
        own_mine[j] = owned(rep * blocks + j) + gf[j]

    receive_all(stage_4, ranks)
    r5[piece] = r4[...].reshape(half_rows, 128).astype(BF16)
    start_all(stage_5, ways)

    for s in range(2):
        near[s][0].wait_recv()
    for s in range(2):
        near[s][1].wait_recv()
    for s in range(2):
        for j in range(part):
            at = s * part + j
            gf[at] = own_mine[at] + got_near[0, 1 - s, j].astype(F32) + got_near[1, s, j].astype(F32)
    gf_copy = pltpu.make_async_copy(gf, gf_hbm, out_sem.at[1])
    gf_copy.start()

    scale = 1.0 / math.sqrt(nodes)
    receive_all(stage_5, ways)
    for c in range(2):
        columns = slice(c * 128, (c + 1) * 128)
        for h in range(2):
            rows = slice(h * half_rows, (h + 1) * half_rows)
            gs_ref[rows, columns] = r5[c * 2 + h].astype(F32) * scale
            gn_ref[rows, columns] = r5[(2 + c) * 2 + h].astype(F32) * scale
        gb_ref[:, columns] = (final_bias[c : c + 1] + final_bias[2 + c : 3 + c]) * scale

    for send in shared + sends + returns:
        send.wait_send()
    for n in range(len(far)):
        for k in range(1, reps):
            hand_on(n, k).wait_send()
            gather_far(n, k).wait_send()
        return_far(n).wait_send()
    for s in range(2):
        passing[s].wait_send()
        for h in range(2):
            near[s][h].wait_send()
    finish_all(stage_1, ways)
    finish_all(stage_2, ranks)
    finish_all(stage_3, layers)
    finish_all(stage_4, ranks)
    finish_all(stage_5, ways)
    act_copy.wait()
    gf_copy.wait()


def write_out(*refs):
    count = (len(refs) - 1) // 3
    given, results, held, sem = refs[:count], refs[count : 2 * count], refs[2 * count : 3 * count], refs[-1]
    reads = [pltpu.make_async_copy(given[i], held[i], sem.at[0, i]) for i in range(count)]
    writes = [pltpu.make_async_copy(held[i], results[i], sem.at[1, i]) for i in range(count)]
    for read in reads:
        read.start()
    for read, write in zip(reads, writes):
        read.wait()
        write.start()
    for write in writes:
        write.wait()


def per_device(sizes, features, w_self, w_neigh, bias, cotangent, slot_source, tile_masks, panel_blocks):
    doms, reps, subs, offsets, nodes = sizes
    layers = doms // subs
    blocks, slots, tile, _ = tile_masks.shape
    width, hidden = w_self.shape
    part_blocks = features.shape[0] // tile
    turns, panel = panel_blocks.shape[1:]
    tiles = blocks * slots // 2
    ways, ranks, half_rows = 2 * reps, subs // 2, width // 2
    rows_each = half_rows // ranks
    part = blocks // 2
    dma = pltpu.SemaphoreType.DMA
    any_space = pl.BlockSpec(memory_space=pl.ANY)
    vmem = pl.BlockSpec(memory_space=pltpu.VMEM)
    smem = pl.BlockSpec(memory_space=pltpu.SMEM)
    block = (tile, width)
    scratch = [
        pltpu.VMEM((part_blocks,) + block, BF16),
        pltpu.VMEM((width, hidden), BF16),
        pltpu.VMEM((width, hidden), BF16),
        pltpu.VMEM((1, hidden), F32),
        pltpu.VMEM((blocks, tile, hidden), BF16),
        pltpu.VMEM((blocks, slots, tile, tile), jnp.int32),
        pltpu.VMEM((blocks, slots, tile, tile), BF16),
        pltpu.VMEM((blocks, slots, tile, tile), BF16),
        pltpu.VMEM((blocks,) + block, F32),
        pltpu.VMEM((blocks, tile, hidden), F32),
        pltpu.VMEM((blocks,) + block, F32),
        pltpu.VMEM((width, blocks * tile), BF16),
        pltpu.VMEM((width, blocks * tile), BF16),
        pltpu.VMEM((blocks, tile, hidden), BF16),
        pltpu.VMEM((blocks,) + block, BF16),
        pltpu.VMEM((blocks, tile, hidden), BF16),
        pltpu.VMEM((blocks,) + block, F32),
        pltpu.VMEM((2 * reps - 2,) + block, BF16),
        pltpu.VMEM((2,) + block, BF16),
        pltpu.VMEM((turns * panel,) + block, BF16),
        pltpu.VMEM((turns * panel,) + block, BF16),
        pltpu.VMEM((turns * panel,) + block, BF16),
        pltpu.VMEM((turns * panel,) + block, BF16),
        pltpu.VMEM((tiles + 1,) + block, F32),
        pltpu.VMEM((tiles + 1,) + block, F32),
        pltpu.VMEM((turns * panel + 1,) + block, F32),
        pltpu.VMEM((2, part) + block, F32),
        pltpu.VMEM((blocks,) + block, F32),
        pltpu.VMEM((2, part) + block, BF16),
        pltpu.VMEM((2, 2, part) + block, BF16),
        pltpu.VMEM((2, part) + block, BF16),
        pltpu.VMEM((2, 2, part) + block, BF16),
        pltpu.VMEM((8, 128), jnp.int32),
        pltpu.SMEM((8, 128), jnp.int32),
        pltpu.VMEM((ways, half_rows + 16, 128), BF16),
        pltpu.VMEM((ways - 1, half_rows + 16, 128), BF16),
        pltpu.VMEM((ranks, rows_each + 8, 128), F32),
        pltpu.VMEM((ranks - 1, rows_each + 8, 128), F32),
        pltpu.VMEM((rows_each + 8, 128), F32),
        pltpu.VMEM((layers - 1, rows_each + 8, 128), F32),
        pltpu.VMEM((ranks, rows_each, 128), F32),
        pltpu.VMEM((ways, half_rows, 128), BF16),
        dma((5,)), dma((blocks,)), dma, dma((2,)),
        dma((turns,)), dma((turns,)), dma((2,)), dma((2,)), dma((2 * reps - 2,)), dma((2 * reps - 2,)),
        dma((2 * reps - 2,)), dma((2 * reps - 2,)), dma((2,)), dma((2,)),
        dma((turns,)), dma((turns,)), dma((6,)), dma((6,)),
        dma((ways - 1,)), dma((ways - 1,)), dma((ranks - 1,)), dma((ranks - 1,)),
        dma((layers - 1,)), dma((layers - 1,)), dma((ranks - 1,)), dma((ranks - 1,)),
        dma((ways - 1,)), dma((ways - 1,)),
    ]
    results = pl.pallas_call(
        functools.partial(kernel, sizes),
        out_shape=(
            jax.ShapeDtypeStruct((blocks, tile, hidden), BF16),
            jax.ShapeDtypeStruct((blocks,) + block, F32),
            jax.ShapeDtypeStruct((width, hidden), F32),
            jax.ShapeDtypeStruct((width, hidden), F32),
            jax.ShapeDtypeStruct((1, hidden), F32),
        ),
        in_specs=[any_space] * 6 + [smem] * 2,
        out_specs=(any_space, any_space, vmem, vmem, vmem),
        scratch_shapes=scratch,
        compiler_params=pltpu.CompilerParams(
            collective_id=0, has_side_effects=True, vmem_limit_bytes=63 * 1024 * 1024
        ),
    )(
        features.reshape((part_blocks,) + block),
        w_self,
        w_neigh,
        bias.reshape(1, hidden),
        cotangent.reshape(blocks, tile, hidden),
        tile_masks,
        slot_source,
        panel_blocks.transpose(1, 0, 2),
    )
    act, gf, gs, gn, gb = pl.pallas_call(
        write_out,
        out_shape=tuple(jax.ShapeDtypeStruct(x.shape, x.dtype) for x in results),
        in_specs=[any_space] * len(results),
        out_specs=(any_space,) * len(results),
        scratch_shapes=[pltpu.VMEM(x.shape, x.dtype) for x in results] + [dma((2, len(results)))],
        compiler_params=pltpu.CompilerParams(vmem_limit_bytes=63 * 1024 * 1024),
    )(*results)
    return (
        act.reshape(blocks * tile, hidden),
        gf.reshape(blocks * tile, width),
        gs,
        gn,
        gb.reshape(hidden),
    )


def solution(mesh):
    doms, reps = mesh.shape["dom"], mesh.shape["rep"]
    subs = 16 if doms % 16 == 0 else doms // 2
    offsets = (1, -1, 2, -2, 3, -3)
    in_specs = (
        P("dom", None),
        P(),
        P(),
        P(),
        P(("dom", "rep"), None),
        P(("dom", "rep"), None),
        P(("dom", "rep"), None, None, None),
        P("dom", None, None),
    )
    out_specs = (P(("dom", "rep"), None), P(("dom", "rep"), None), P(), P(), P())

    def step(features, *rest):
        nodes = features.shape[0] * doms
        return per_device((doms, reps, subs, offsets, nodes), features, *rest)

    return jax.shard_map(step, mesh=mesh, in_specs=in_specs, out_specs=out_specs, check_vma=False)
```
